512 devices in a mesh: gx: 16 (over x, y_hi), gy: 32 (over z, y_lo, core).
Axes of the slice: x: 4, y: 8 (y_hi: 4, y_lo: 2; y = y_hi * 2 + y_lo), z: 8, core: 2. Of those that a mesh axis runs over, the one named last changes fastest.
Arguments:
- spectra: bfloat16 [114688, 1024], P(('gx', 'gy')), may hold values from -16 to 16
- scores: bfloat16 [114688, 32], P(('gx', 'gy')), may hold values from -0.5 to 1.5
Outputs:
- product: float32 [114688, 32], P(('gx', 'gy'))
The draws below stay inside these ranges and needn't reach their ends.
All inputs are finite; a program needn't handle non-finite values.
Results may differ from the reference program's by a relative error of at most 0.0003.
Values may be sent and summed in bfloat16 or wider, within the bound.
No kernel may reach another device: no remote copies, remote signals or barrier semaphores. Data moves between devices by JAX's collectives and lax.ppermute only.
A program may use at most 64 MiB of HBM per device.

```python
import math
import jax
import jax.numpy as jnp
from jax import lax

WAVE = 1024
COLS = 32
BLK = 224
ROUNDS = 16
SPECTRA = 114688


def draw_spectra(key, part):
    key = jax.random.fold_in(key, 11)
    keys = jax.random.split(key, 5)
    bands = 32
    index = jnp.arange(bands, dtype=jnp.float32)
    rate = 0.01 * 150.0 ** ((index + 0.5) / bands)
    loading_scale = jnp.sqrt(rate / 8.0)
    centre = jax.random.uniform(keys[0], (bands,), jnp.float32, 0.1, 0.9)
    width = jnp.exp(jax.random.uniform(keys[1], (bands,), jnp.float32, math.log(0.02), math.log(0.12)))
    position = (jnp.arange(WAVE, dtype=jnp.float32) + 0.5) / WAVE
    envelope = jnp.exp(-0.5 * jnp.square((position[None, :] - centre[:, None]) / width[:, None]))
    texture = 0.5 + jax.random.uniform(keys[2], (bands, WAVE), jnp.float32)
    shapes = envelope * texture / jnp.sqrt(width[:, None] * math.sqrt(math.pi) * 13.0 / 12.0)
    factors = jnp.clip(jax.random.normal(keys[3], (SPECTRA, bands), jnp.float32), -4.0, 4.0)
    noise = 0.5 * jnp.clip(jax.random.normal(keys[4], (SPECTRA, WAVE), jnp.float32), -4.0, 4.0)
    total = noise
    for band in range(bands):
        total = total + factors[:, band:band + 1] * loading_scale[band] * shapes[band][None, :]
    return jnp.clip(total, -16.0, 16.0).astype(jnp.bfloat16)


def shard_levels(stream_key, dims, shards, low, largest):
    factor_of, own = 1.0, jax.random.fold_in(stream_key, 6)
    for dim, parts in shards:
        steps = jnp.exp(jax.random.uniform(jax.random.fold_in(own, dim), (parts,), jnp.float32, low / len(shards), largest / len(shards)))
        factor_of = factor_of * jnp.repeat(steps, dims[dim] // parts).reshape([-1 if axis == dim else 1 for axis in range(len(dims))])
    return factor_of


def setup_inputs(seed: int = 0) -> dict:
    arg_keys = jax.random.split(jax.random.key(seed), 3)
    spectra = draw_spectra(jax.random.fold_in(arg_keys[2], 71), 0)
    scores = jnp.clip(-0.5 + 2.0 * jax.random.uniform(arg_keys[1], (SPECTRA, COLS), jnp.float32) ** shard_levels(arg_keys[1], (SPECTRA, COLS), ((0, 512),), -0.2, 0.2), -0.5, 1.5).astype(jnp.bfloat16)
    return dict(spectra=spectra, scores=scores)


spread_rate = 4.0


def kernel_tile(rows_x, rows_sq, cols_x, cols_sq):
    cross = jnp.dot(rows_x, cols_x.T, preferred_element_type=jnp.float32)
    dist = rows_sq[:, None] + cols_sq[None, :] - 2.0 * cross
    return jnp.exp(-spread_rate * dist / WAVE).astype(jnp.bfloat16)


def reference(spectra, scores):
    blocks = SPECTRA // BLK
    sq_all = jnp.sum(jnp.square(spectra.astype(jnp.float32)), axis=1)
    spec_blocks = spectra.reshape(blocks, BLK, WAVE)
    score_blocks = scores.reshape(blocks, BLK, COLS)
    sq_blocks = sq_all.reshape(blocks, BLK)

    def one_block(home):
        home_x = lax.dynamic_index_in_dim(spec_blocks, home, keepdims=False)
        home_sq = lax.dynamic_index_in_dim(sq_blocks, home, keepdims=False)
        home_u = lax.dynamic_index_in_dim(score_blocks, home, keepdims=False)
        near = jnp.zeros((BLK, COLS), jnp.float32)
        backward = []
        for offset in range(ROUNDS + 1):
            other = ((home + offset) % blocks).astype(jnp.int32)
            other_x = lax.dynamic_index_in_dim(spec_blocks, other, keepdims=False)
            other_sq = lax.dynamic_index_in_dim(sq_blocks, other, keepdims=False)
            other_u = lax.dynamic_index_in_dim(score_blocks, other, keepdims=False)
            kern = kernel_tile(home_x, home_sq, other_x, other_sq)
            near = near + jnp.dot(kern, other_u, preferred_element_type=jnp.float32)
            if offset > 0:
                backward.append(jnp.dot(kern.T, home_u, preferred_element_type=jnp.float32))
        return near, jnp.stack(backward)

    near_all, far_all = lax.map(one_block, jnp.arange(blocks, dtype=jnp.int32))
    total = near_all
    for offset in range(1, ROUNDS + 1):
        total = total + jnp.roll(far_all[:, offset - 1], offset, axis=0)
    return total.reshape(SPECTRA, COLS)
```

```python
import functools

import jax
import jax.numpy as jnp
from jax import lax
from jax.experimental import pallas as pl
from jax.experimental.pallas import tpu as pltpu
from jax.sharding import PartitionSpec as P

WAVE = 1024
BLK = 224
COLS = 32
PACK = 16
AXES = ("gx", "gy")

spread_rate = 4.0


def split(i):
    return i >> 2, (i >> 1) & 1, i & 1


def device(quad, side, core, quads):
    return (quad % quads) * 4 + side * 2 + core


def stepped(i, j, quads):
    quad, side, core = split(i)
    return device(quad + (j if side == 0 else -j), side, core, quads)


def first_partner(i, quads):
    quad, side, core = split(i)
    other = {(0, 0): (1, 0), (1, 1): (0, 0), (0, 1): (1, 1), (1, 0): (0, 1)}[(side, core)]
    return device(quad, *other, quads)


def second_partner(i, quads):
    quad, side, core = split(i)
    other = {(1, 0): (0, 0), (0, 1): (1, 0), (1, 1): (0, 1), (0, 0): (1, 1)}[(side, core)]
    return device(quad, *other, quads)


def fetch(block, source, n):
    return lax.ppermute(block, AXES, [(source(i), i) for i in range(n)])


def give(block, target, n):
    return lax.ppermute(block, AXES, [(i, target(i)) for i in range(n)])


def packed(spectra, scores):
    turned = scores.T
    both = jnp.concatenate(
        [jnp.pad(turned[:PACK], ((0, 0), (0, 32))), jnp.pad(turned[PACK:], ((0, 0), (0, WAVE - 256 - BLK)))], axis=1
    )
    return jnp.concatenate([spectra, both], axis=0)


def rows_of(ref):
    return ref[0:BLK, :]


def scores_of(ref):
    return jnp.concatenate([ref[BLK:BLK + PACK, 0:BLK], ref[BLK:BLK + PACK, 256:256 + BLK]], axis=0)


def norms_of(ref):
    x = rows_of(ref).astype(jnp.float32)
    column = jnp.sum(x * x, axis=1, keepdims=True)
    row = jnp.broadcast_to(column, (BLK, 128)).T[0:1, :]
    return column, row


def tile_of(a_ref, a_column, b_ref, b_row):
    cross = lax.dot_general(
        rows_of(a_ref), rows_of(b_ref), (((1,), (1,)), ((), ())), preferred_element_type=jnp.float32
    )
    dist = a_column + b_row - 2.0 * cross
    return jnp.exp(-spread_rate * dist / WAVE).astype(jnp.bfloat16)


def to_rows(kern, b_scores):
    return lax.dot_general(b_scores, kern, (((1,), (1,)), ((), ())), preferred_element_type=jnp.float32)


def to_columns(kern, a_scores):
    return jnp.dot(a_scores, kern, preferred_element_type=jnp.float32)


def pairs_body(tiles, outs, *refs):
    blocks, totals = refs[:len(refs) - len(outs)], refs[len(refs) - len(outs):]
    used = sorted({t for tile in tiles for t in tile})
    norms = {t: norms_of(blocks[t]) for t in used}
    scores = {t: scores_of(blocks[t]) for t in used}
    sums = {}

    def add(t, value):
        sums[t] = value if t not in sums else sums[t] + value

    for a, b in tiles:
        kern = tile_of(blocks[a], norms[a][0], blocks[b], norms[b][1])
        add(a, to_rows(kern, scores[b]))
        if a != b:
            add(b, to_columns(kern, scores[a]))
    for t, total in zip(outs, totals):
        total[...] = sums[t]


VMEM = pl.BlockSpec(memory_space=pltpu.VMEM)


def cost(tiles, blocks):
    return pl.CostEstimate(
        flops=tiles * 2 * BLK * BLK * (WAVE + 2 * COLS),
        bytes_accessed=blocks * (BLK + PACK) * WAVE * 2,
        transcendentals=tiles * BLK * BLK,
    )


def pairs(blocks, tiles, outs):
    return pl.pallas_call(
        functools.partial(pairs_body, tiles, outs),
        out_shape=[jax.ShapeDtypeStruct((COLS, BLK), jnp.float32)] * len(outs),
        in_specs=[VMEM] * len(blocks),
        out_specs=[VMEM] * len(outs),
        compiler_params=pltpu.CompilerParams(vmem_limit_bytes=24 * 1024 * 1024),
        cost_estimate=cost(len(tiles), len(blocks)),
    )(*blocks)


def sibling_body(kind_ref, extra_ref, zero_ref, up_ref, down_ref, up2_ref, down2_ref, *totals):
    extra_total, zero_total, up_total, down_total, up2_total, down2_total = totals
    column, _ = norms_of(extra_ref)
    extra_scores = scores_of(extra_ref)

    def one(ref):
        kern = tile_of(extra_ref, column, ref, norms_of(ref)[1])
        return to_rows(kern, scores_of(ref)), to_columns(kern, extra_scores)

    total, zero_total[...] = one(zero_ref)
    mine, up_total[...] = one(up_ref)
    total = total + mine
    mine, down_total[...] = one(down_ref)
    extra_total[...] = total + mine

    @pl.when(kind_ref[0] == 0)
    def _():
        value, up2_total[...] = one(up2_ref)
        extra_total[...] += value
        down2_total[...] = jnp.zeros_like(down2_total)

    @pl.when(kind_ref[0] != 0)
    def _():
        value, down2_total[...] = one(down2_ref)
        extra_total[...] += value
        up2_total[...] = jnp.zeros_like(up2_total)


def sibling_pairs(kind, blocks):
    return pl.pallas_call(
        sibling_body,
        out_shape=[jax.ShapeDtypeStruct((COLS, BLK), jnp.float32)] * 6,
        in_specs=[pl.BlockSpec(memory_space=pltpu.SMEM)] + [VMEM] * 6,
        out_specs=[VMEM] * 6,
        compiler_params=pltpu.CompilerParams(vmem_limit_bytes=24 * 1024 * 1024),
        cost_estimate=cost(4, 6),
    )(kind, *blocks)


def on_device(spectra, scores):
    n = lax.axis_size(AXES)
    quads = n // 4
    me = lax.axis_index(AXES)
    kind = (((me >> 1) ^ me) & 1).astype(jnp.int32).reshape(1)

    zero = packed(spectra, scores)
    up = fetch(zero, lambda i: stepped(i, 1, quads), n)
    down = fetch(zero, lambda i: stepped(i, -1, quads), n)
    up2 = fetch(up, lambda i: stepped(i, 1, quads), n)
    down2 = fetch(down, lambda i: stepped(i, -1, quads), n)
    first = fetch(down, lambda i: first_partner(i, quads), n)
    sibling = fetch(up2, lambda i: i ^ 1, n)
    second = fetch(up2, lambda i: second_partner(i, quads), n)

    a0, a1, a9 = pairs([zero, up, down], ((0, 0), (0, 1), (2, 1)), (0, 1, 2))
    b0, b1, b9, b2, b8, bf = pairs(
        [zero, up, down, up2, down2, first],
        ((2, 3), (4, 3), (5, 0), (5, 1), (5, 2), (5, 3), (5, 4)),
        (0, 1, 2, 3, 4, 5),
    )
    df, d0, d1, d9, d2, d8 = sibling_pairs(kind, [sibling, zero, up, down, up2, down2])
    c0, c1, c2, cs = pairs([zero, up, up2, second], ((3, 0), (3, 1), (3, 2)), (0, 1, 2, 3))

    def home_of_first(i):
        return stepped(first_partner(i, quads), -1, quads)

    def home_of_sibling(i):
        return stepped(i ^ 1, 2, quads)

    def home_of_second(i):
        return stepped(second_partner(i, quads), 2, quads)

    total = a0 + b0 + d0 + c0
    total = total + give(bf, home_of_first, n)
    total = total + give(a9 + b9 + d9, lambda i: stepped(i, -1, quads), n)
    total = total + give(b8 + d8, lambda i: stepped(i, -2, quads), n)
    total = total + give(df, home_of_sibling, n)
    total = total + give(cs, home_of_second, n)
    total = total + give(a1 + b1 + d1 + c1, lambda i: stepped(i, 1, quads), n)
    total = total + give(b2 + d2 + c2, lambda i: stepped(i, 2, quads), n)
    return total.T


def solution(mesh):
    return jax.shard_map(
        on_device,
        mesh=mesh,
        in_specs=(P(AXES, None), P(AXES, None)),
        out_specs=P(AXES, None),
        check_vma=False,
    )
```

```python
import functools

import jax
import jax.numpy as jnp
from jax import lax
from jax.experimental import pallas as pl
from jax.experimental.pallas import tpu as pltpu
from jax.sharding import PartitionSpec as P

WAVE = 1024
BLK = 224
COLS = 32
PACK = 16
AXES = ("gx", "gy")

spread_rate = 4.0


def split(i):
    return i >> 2, (i >> 1) & 1, i & 1


def device(quad, side, core, quads):
    return (quad % quads) * 4 + side * 2 + core


def stepped(i, j, quads):
    quad, side, core = split(i)
    return device(quad + (j if side == 0 else -j), side, core, quads)


def first_partner(i, quads):
    quad, side, core = split(i)
    other = {(0, 0): (1, 0), (1, 1): (0, 0), (0, 1): (1, 1), (1, 0): (0, 1)}[(side, core)]
    return device(quad, *other, quads)


def second_partner(i, quads):
    quad, side, core = split(i)
    other = {(1, 0): (0, 0), (0, 1): (1, 0), (1, 1): (0, 1), (0, 0): (1, 1)}[(side, core)]
    return device(quad, *other, quads)


def fetch(block, source, n):
    return lax.ppermute(block, AXES, [(source(i), i) for i in range(n)])


def give(block, target, n):
    return lax.ppermute(block, AXES, [(i, target(i)) for i in range(n)])


def packed(spectra, scores):
    turned = scores.T
    both = jnp.concatenate(
        [jnp.pad(turned[:PACK], ((0, 0), (0, 32))), jnp.pad(turned[PACK:], ((0, 0), (0, WAVE - 256 - BLK)))], axis=1
    )
    return jnp.concatenate([spectra, both], axis=0)


def rows_of(ref):
    return ref[0:BLK, :]


def scores_of(ref):
    return jnp.concatenate([ref[BLK:BLK + PACK, 0:BLK], ref[BLK:BLK + PACK, 256:256 + BLK]], axis=0)


def norms_of(ref):
    x = rows_of(ref).astype(jnp.float32)
    column = jnp.sum(x * x, axis=1, keepdims=True)
    row = jnp.broadcast_to(column, (BLK, 128)).T[0:1, :]
    return column, row


def tile_of(a_ref, a_column, b_ref, b_row):
    cross = lax.dot_general(
        rows_of(a_ref), rows_of(b_ref), (((1,), (1,)), ((), ())), preferred_element_type=jnp.float32
    )
    dist = a_column + b_row - 2.0 * cross
    return jnp.exp(-spread_rate * dist / WAVE).astype(jnp.bfloat16)


def to_rows(kern, b_scores):
    return lax.dot_general(b_scores, kern, (((1,), (1,)), ((), ())), preferred_element_type=jnp.float32)


def to_columns(kern, a_scores):
    return jnp.dot(a_scores, kern, preferred_element_type=jnp.float32)


def pairs_body(tiles, outs, *refs):
    blocks, totals = refs[:len(refs) - len(outs)], refs[len(refs) - len(outs):]
    used = sorted({t for tile in tiles for t in tile})
    norms = {t: norms_of(blocks[t]) for t in used}
    scores = {t: scores_of(blocks[t]) for t in used}
    sums = {}

    def add(t, value):
        sums[t] = value if t not in sums else sums[t] + value

    for a, b in tiles:
        kern = tile_of(blocks[a], norms[a][0], blocks[b], norms[b][1])
        add(a, to_rows(kern, scores[b]))
        if a != b:
            add(b, to_columns(kern, scores[a]))
    for t, total in zip(outs, totals):
        total[...] = sums[t]


VMEM = pl.BlockSpec(memory_space=pltpu.VMEM)


def cost(tiles, blocks):
    return pl.CostEstimate(
        flops=tiles * 2 * BLK * BLK * (WAVE + 2 * COLS),
        bytes_accessed=blocks * (BLK + PACK) * WAVE * 2,
        transcendentals=tiles * BLK * BLK,
    )


def pairs(blocks, tiles, outs):
    return pl.pallas_call(
        functools.partial(pairs_body, tiles, outs),
        out_shape=[jax.ShapeDtypeStruct((COLS, BLK), jnp.float32)] * len(outs),
        in_specs=[VMEM] * len(blocks),
        out_specs=[VMEM] * len(outs),
        compiler_params=pltpu.CompilerParams(vmem_limit_bytes=24 * 1024 * 1024),
        cost_estimate=cost(len(tiles), len(blocks)),
    )(*blocks)


def sibling_body(kind_ref, extra_ref, zero_ref, up_ref, down_ref, up2_ref, down2_ref, *totals):
    extra_total, zero_total, up_total, down_total, up2_total, down2_total = totals
    column, _ = norms_of(extra_ref)
    extra_scores = scores_of(extra_ref)

    def one(ref):
        kern = tile_of(extra_ref, column, ref, norms_of(ref)[1])
        return to_rows(kern, scores_of(ref)), to_columns(kern, extra_scores)

    total, zero_total[...] = one(zero_ref)
    mine, up_total[...] = one(up_ref)
    total = total + mine
    mine, down_total[...] = one(down_ref)
    extra_total[...] = total + mine

    @pl.when(kind_ref[0] == 0)
    def _():
        value, up2_total[...] = one(up2_ref)
        extra_total[...] += value
        down2_total[...] = jnp.zeros_like(down2_total)

    @pl.when(kind_ref[0] != 0)
    def _():
        value, down2_total[...] = one(down2_ref)
        extra_total[...] += value
        up2_total[...] = jnp.zeros_like(up2_total)


def sibling_pairs(kind, blocks):
    return pl.pallas_call(
        sibling_body,
        out_shape=[jax.ShapeDtypeStruct((COLS, BLK), jnp.float32)] * 6,
        in_specs=[pl.BlockSpec(memory_space=pltpu.SMEM)] + [VMEM] * 6,
        out_specs=[VMEM] * 6,
        compiler_params=pltpu.CompilerParams(vmem_limit_bytes=24 * 1024 * 1024),
        cost_estimate=cost(4, 6),
    )(kind, *blocks)


def on_device(spectra, scores):
    n = lax.axis_size(AXES)
    quads = n // 4
    me = lax.axis_index(AXES)
    kind = (((me >> 1) ^ me) & 1).astype(jnp.int32).reshape(1)

    column = lax.axis_size("gy") // 4
    level = (me >> 2) % column
    outer = (level == 0) | (level == column - 1)
    crossing = outer & ((me & 1) == 1)
    leaves_up = (level == column - 1) == (((me >> 1) & 1) == 0)

    def level_of(i):
        return (i >> 2) % column

    def turned(i, j):
        quad, side, core = split(i)
        base = quad - quad % column
        return device(base + (quad - base + (j if side == 0 else -j)) % column, side, core, quads)

    def outer_of(i):
        return i % 2 == 1 and level_of(i) in (0, column - 1)

    def wraps(i, j):
        return stepped(i, j, quads) != turned(i, j)

    def beside(i):
        quad, side, core = split(i)
        return device(quad + (column if level_of(i) else -column), side, core, quads)

    def opposite(i):
        return turned(i, 1) if wraps(i, 1) else turned(i, -1)

    def chosen(pairs_of):
        return [(source, i) for i, source in ((i, pairs_of(i)) for i in range(n)) if source is not None]

    def hop(block, j):
        return lax.ppermute(block, AXES, chosen(lambda i: turned(i, j) if i % 2 else stepped(i, j, quads)))

    def hop_inside(block, j):
        return lax.ppermute(
            block, AXES, chosen(lambda i: None if i % 2 and wraps(i, j) else stepped(i, j, quads))
        )

    def across(block):
        return lax.ppermute(block, AXES, chosen(lambda i: beside(i) if outer_of(i) else None))

    def through(block):
        return lax.ppermute(block, AXES, chosen(lambda i: opposite(i) if outer_of(i) else None))

    zero = packed(spectra, scores)
    up = hop(zero, 1)
    down = hop(zero, -1)
    moved = across(jnp.where(leaves_up, up, down))
    later = through(jnp.where(leaves_up, down, up))
    up = jnp.where(crossing & leaves_up, moved, up)
    down = jnp.where(crossing & ~leaves_up, moved, down)
    up2 = hop_inside(up, 1)
    down2 = hop_inside(down, -1)
    later = across(later)
    up2 = jnp.where(crossing & leaves_up, later, up2)
    down2 = jnp.where(crossing & ~leaves_up, later, down2)
    first = fetch(down, lambda i: first_partner(i, quads), n)
    sibling = fetch(up2, lambda i: i ^ 1, n)
    second = fetch(up2, lambda i: second_partner(i, quads), n)

    a0, a1, a9 = pairs([zero, up, down], ((0, 0), (0, 1), (2, 1)), (0, 1, 2))
    b0, b1, b9, b2, b8, bf = pairs(
        [zero, up, down, up2, down2, first],
        ((2, 3), (4, 3), (5, 0), (5, 1), (5, 2), (5, 3), (5, 4)),
        (0, 1, 2, 3, 4, 5),
    )
    df, d0, d1, d9, d2, d8 = sibling_pairs(kind, [sibling, zero, up, down, up2, down2])
    c0, c1, c2, cs = pairs([zero, up, up2, second], ((3, 0), (3, 1), (3, 2)), (0, 1, 2, 3))

    def home_of_first(i):
        return stepped(first_partner(i, quads), -1, quads)

    def home_of_sibling(i):
        return stepped(i ^ 1, 2, quads)

    def home_of_second(i):
        return stepped(second_partner(i, quads), 2, quads)

    total = a0 + b0 + d0 + c0
    total = total + give(bf, home_of_first, n)
    total = total + give(a9 + b9 + d9, lambda i: stepped(i, -1, quads), n)
    total = total + give(b8 + d8, lambda i: stepped(i, -2, quads), n)
    total = total + give(df, home_of_sibling, n)
    total = total + give(cs, home_of_second, n)
    total = total + give(a1 + b1 + d1 + c1, lambda i: stepped(i, 1, quads), n)
    total = total + give(b2 + d2 + c2, lambda i: stepped(i, 2, quads), n)
    return total.T


def solution(mesh):
    return jax.shard_map(
        on_device,
        mesh=mesh,
        in_specs=(P(AXES, None), P(AXES, None)),
        out_specs=P(AXES, None),
        check_vma=False,
    )
```

```python
import functools

import jax
import jax.numpy as jnp
from jax import lax
from jax.experimental import pallas as pl
from jax.experimental.pallas import tpu as pltpu
from jax.sharding import PartitionSpec as P

WAVE = 1024
BLK = 224
COLS = 32
PACK = 16
AXES = ("gx", "gy")

spread_rate = 4.0


def split(i):
    return i >> 2, (i >> 1) & 1, i & 1


def device(quad, side, core, quads):
    return (quad % quads) * 4 + side * 2 + core


def stepped(i, j, quads):
    quad, side, core = split(i)
    return device(quad + (j if side == 0 else -j), side, core, quads)


def first_partner(i, quads):
    quad, side, core = split(i)
    other = {(0, 0): (1, 0), (1, 1): (0, 0), (0, 1): (1, 1), (1, 0): (0, 1)}[(side, core)]
    return device(quad, *other, quads)


def second_partner(i, quads):
    quad, side, core = split(i)
    other = {(1, 0): (0, 0), (0, 1): (1, 0), (1, 1): (0, 1), (0, 0): (1, 1)}[(side, core)]
    return device(quad, *other, quads)


def within(i, j, column, quads):
    return stepped(i, j, quads) // (4 * column) == i // (4 * column)


def near_source(i, j, steps, column, quads):
    return stepped(i, j, quads) if within(i, j * steps, column, quads) else None


def far_source(i, column, quads):
    for j in (2, -2):
        if not within(i, j, column, quads):
            return stepped(i, j, quads)
    return None


def back_level(me, column):
    level = (me >> 2) % column
    return (level == 1) | (level == column - 2)


def back_source(i, column, quads):
    for j in (1, -1):
        if not within(i, j, column, quads):
            return stepped(i, -j, quads)
    return None


def sources(source_of, n, column):
    found = [(source_of(i, column, n // 4), i) for i in range(n)]
    return [(source, i) for source, i in found if source is not None]


def fetch(block, source, n):
    return lax.ppermute(block, AXES, [(source(i), i) for i in range(n)])


def give(block, target, n):
    return lax.ppermute(block, AXES, [(i, target(i)) for i in range(n)])


def packed(spectra, scores):
    turned = scores.T
    both = jnp.concatenate(
        [jnp.pad(turned[:PACK], ((0, 0), (0, 32))), jnp.pad(turned[PACK:], ((0, 0), (0, WAVE - 256 - BLK)))], axis=1
    )
    return jnp.concatenate([spectra, both], axis=0)


def rows_of(ref):
    return ref[0:BLK, :]


def scores_of(ref):
    return jnp.concatenate([ref[BLK:BLK + PACK, 0:BLK], ref[BLK:BLK + PACK, 256:256 + BLK]], axis=0)


def norms_of(ref):
    x = rows_of(ref).astype(jnp.float32)
    column = jnp.sum(x * x, axis=1, keepdims=True)
    row = jnp.broadcast_to(column, (BLK, 128)).T[0:1, :]
    return column, row


def tile_of(a_ref, a_column, b_ref, b_row):
    cross = lax.dot_general(
        rows_of(a_ref), rows_of(b_ref), (((1,), (1,)), ((), ())), preferred_element_type=jnp.float32
    )
    dist = a_column + b_row - 2.0 * cross
    return jnp.exp(-spread_rate * dist / WAVE).astype(jnp.bfloat16)


def to_rows(kern, b_scores):
    return lax.dot_general(b_scores, kern, (((1,), (1,)), ((), ())), preferred_element_type=jnp.float32)


def to_columns(kern, a_scores):
    return jnp.dot(a_scores, kern, preferred_element_type=jnp.float32)


def pairs_body(tiles, outs, *refs):
    blocks, totals = refs[:len(refs) - len(outs)], refs[len(refs) - len(outs):]
    used = sorted({t for tile in tiles for t in tile})
    norms = {t: norms_of(blocks[t]) for t in used}
    scores = {t: scores_of(blocks[t]) for t in used}
    sums = {}

    def add(t, value):
        sums[t] = value if t not in sums else sums[t] + value

    for a, b in tiles:
        kern = tile_of(blocks[a], norms[a][0], blocks[b], norms[b][1])
        add(a, to_rows(kern, scores[b]))
        if a != b:
            add(b, to_columns(kern, scores[a]))
    for t, total in zip(outs, totals):
        total[...] = sums[t]


VMEM = pl.BlockSpec(memory_space=pltpu.VMEM)


def cost(tiles, blocks):
    return pl.CostEstimate(
        flops=tiles * 2 * BLK * BLK * (WAVE + 2 * COLS),
        bytes_accessed=blocks * (BLK + PACK) * WAVE * 2,
        transcendentals=tiles * BLK * BLK,
    )


def pairs(blocks, tiles, outs):
    return pl.pallas_call(
        functools.partial(pairs_body, tiles, outs),
        out_shape=[jax.ShapeDtypeStruct((COLS, BLK), jnp.float32)] * len(outs),
        in_specs=[VMEM] * len(blocks),
        out_specs=[VMEM] * len(outs),
        compiler_params=pltpu.CompilerParams(vmem_limit_bytes=24 * 1024 * 1024),
        cost_estimate=cost(len(tiles), len(blocks)),
    )(*blocks)


def sibling_body(kind_ref, extra_ref, zero_ref, up_ref, down_ref, up2_ref, down2_ref, *totals):
    extra_total, zero_total, up_total, down_total, up2_total, down2_total = totals
    column, _ = norms_of(extra_ref)
    extra_scores = scores_of(extra_ref)

    def one(ref):
        kern = tile_of(extra_ref, column, ref, norms_of(ref)[1])
        return to_rows(kern, scores_of(ref)), to_columns(kern, extra_scores)

    total, zero_total[...] = one(zero_ref)
    mine, up_total[...] = one(up_ref)
    total = total + mine
    mine, down_total[...] = one(down_ref)
    extra_total[...] = total + mine

    @pl.when(kind_ref[0] == 0)
    def _():
        value, up2_total[...] = one(up2_ref)
        extra_total[...] += value
        down2_total[...] = jnp.zeros_like(down2_total)

    @pl.when(kind_ref[0] != 0)
    def _():
        value, down2_total[...] = one(down2_ref)
        extra_total[...] += value
        up2_total[...] = jnp.zeros_like(up2_total)


def sibling_pairs(kind, blocks):
    return pl.pallas_call(
        sibling_body,
        out_shape=[jax.ShapeDtypeStruct((COLS, BLK), jnp.float32)] * 6,
        in_specs=[pl.BlockSpec(memory_space=pltpu.SMEM)] + [VMEM] * 6,
        out_specs=[VMEM] * 6,
        compiler_params=pltpu.CompilerParams(vmem_limit_bytes=24 * 1024 * 1024),
        cost_estimate=cost(4, 6),
    )(kind, *blocks)


def on_device(spectra, scores):
    n = lax.axis_size(AXES)
    quads = n // 4
    me = lax.axis_index(AXES)
    kind = (((me >> 1) ^ me) & 1).astype(jnp.int32).reshape(1)

    column = lax.axis_size("gy") // 4
    level = (me >> 2) % column
    side = (me >> 1) & 1
    low, high = level < 2, level >= column - 2
    far_up = jnp.where(side == 0, high, low)
    far_down = jnp.where(side == 0, low, high)
    back_up = level == jnp.where(side == 0, column - 1, 0)
    back_down = level == jnp.where(side == 0, 0, column - 1)

    def route(block, source_of):
        return lax.ppermute(block, AXES, sources(source_of, n, column))

    zero = packed(spectra, scores)
    far = route(zero, far_source)
    up = route(zero, lambda i, column, quads: near_source(i, 1, 1, column, quads))
    down = route(zero, lambda i, column, quads: near_source(i, -1, 1, column, quads))
    up2 = route(up, lambda i, column, quads: near_source(i, 1, 2, column, quads))
    down2 = route(down, lambda i, column, quads: near_source(i, -1, 2, column, quads))
    edge = back_level(me, column)
    back = route(jnp.where(edge, far, jnp.where(side == 0, up, down)), back_source)
    up2 = jnp.where(far_up, far, up2)
    down2 = jnp.where(far_down, far, down2)
    back, _, _ = lax.optimization_barrier((back, up2, down2))
    up = jnp.where(back_up, back, up)
    down = jnp.where(back_down, back, down)
    sibling = fetch(up2, lambda i: i ^ 1, n)
    second = fetch(up2, lambda i: second_partner(i, quads), n)
    first = fetch(jnp.where(me < n, down, up2), lambda i: first_partner(i, quads), n)

    a0, a1, a9 = pairs([zero, up, down], ((0, 0), (0, 1), (2, 1)), (0, 1, 2))
    b0, b1, b9, b2, b8, bs = pairs(
        [zero, up, down, up2, down2, second],
        ((2, 3), (4, 3), (5, 0), (5, 1), (5, 2), (5, 3), (5, 4)),
        (0, 1, 2, 3, 4, 5),
    )
    df, d0, d1, d9, d2, d8 = sibling_pairs(kind, [sibling, zero, up, down, up2, down2])
    c0, c9, c8, cf = pairs([zero, down, down2, first], ((3, 0), (3, 1), (3, 2)), (0, 1, 2, 3))

    def home_of_first(i):
        return stepped(first_partner(i, quads), -1, quads)

    def home_of_sibling(i):
        return stepped(i ^ 1, 2, quads)

    def home_of_second(i):
        return stepped(second_partner(i, quads), 2, quads)

    total = a0 + b0 + d0 + c0
    total = total + give(bs, home_of_second, n)
    total = total + give(a1 + b1 + d1, lambda i: stepped(i, 1, quads), n)
    total = total + give(b2 + d2, lambda i: stepped(i, 2, quads), n)
    total = total + give(df, home_of_sibling, n)
    total = total + give(cf, home_of_first, n)
    total = total + give(a9 + b9 + d9 + c9, lambda i: stepped(i, -1, quads), n)
    total = total + give(b8 + d8 + c8, lambda i: stepped(i, -2, quads), n)
    return total.T


def solution(mesh):
    return jax.shard_map(
        on_device,
        mesh=mesh,
        in_specs=(P(AXES, None), P(AXES, None)),
        out_specs=P(AXES, None),
        check_vma=False,
    )
```

```python
import functools

import jax
import jax.numpy as jnp
from jax import lax
from jax.experimental import pallas as pl
from jax.experimental.pallas import tpu as pltpu
from jax.sharding import PartitionSpec as P

WAVE = 1024
BLK = 224
COLS = 32
PACK = 16
AXES = ("gx", "gy")

spread_rate = 4.0


def split(i):
    return i >> 2, (i >> 1) & 1, i & 1


def device(quad, side, core, quads):
    return (quad % quads) * 4 + side * 2 + core


def stepped(i, j, quads):
    quad, side, core = split(i)
    return device(quad + (j if side == 0 else -j), side, core, quads)


def first_partner(i, quads):
    quad, side, core = split(i)
    other = {(0, 0): (1, 0), (1, 1): (0, 0), (0, 1): (1, 1), (1, 0): (0, 1)}[(side, core)]
    return device(quad, *other, quads)


def second_partner(i, quads):
    quad, side, core = split(i)
    other = {(1, 0): (0, 0), (0, 1): (1, 0), (1, 1): (0, 1), (0, 0): (1, 1)}[(side, core)]
    return device(quad, *other, quads)


def within(i, j, column, quads):
    return stepped(i, j, quads) // (4 * column) == i // (4 * column)


def near_source(i, j, steps, column, quads):
    return stepped(i, j, quads) if within(i, j * steps, column, quads) else None


def inner_source(i, j, column, quads):
    return stepped(i, j, quads) if within(i, j, column, quads) else None


def far_source(i, column, quads):
    for j in (2, -2):
        if not within(i, j, column, quads):
            return stepped(i, j, quads)
    return None


def back_level(me, column):
    level = (me >> 2) % column
    return (level == 1) | (level == column - 2)


def back_source(i, column, quads):
    for j in (1, -1):
        if not within(i, j, column, quads):
            return stepped(i, -j, quads)
    return None


def sources(source_of, n, column):
    found = [(source_of(i, column, n // 4), i) for i in range(n)]
    return [(source, i) for source, i in found if source is not None]


def fetch(block, source, n):
    return lax.ppermute(block, AXES, [(source(i), i) for i in range(n)])


def give(block, target, n):
    return lax.ppermute(block, AXES, [(i, target(i)) for i in range(n)])


def packed(spectra, scores):
    turned = scores.T
    both = jnp.concatenate(
        [jnp.pad(turned[:PACK], ((0, 0), (0, 32))), jnp.pad(turned[PACK:], ((0, 0), (0, WAVE - 256 - BLK)))], axis=1
    )
    return jnp.concatenate([spectra, both], axis=0)


def rows_of(ref):
    return ref[0:BLK, :]


def scores_of(ref):
    return jnp.concatenate([ref[BLK:BLK + PACK, 0:BLK], ref[BLK:BLK + PACK, 256:256 + BLK]], axis=0)


def norms_of(ref):
    x = rows_of(ref).astype(jnp.float32)
    column = jnp.sum(x * x, axis=1, keepdims=True)
    row = jnp.broadcast_to(column, (BLK, 128)).T[0:1, :]
    return column, row


def tile_of(a_ref, a_column, b_ref, b_row):
    cross = lax.dot_general(
        rows_of(a_ref), rows_of(b_ref), (((1,), (1,)), ((), ())), preferred_element_type=jnp.float32
    )
    dist = a_column + b_row - 2.0 * cross
    return jnp.exp(-spread_rate * dist / WAVE).astype(jnp.bfloat16)


def to_rows(kern, b_scores):
    return lax.dot_general(b_scores, kern, (((1,), (1,)), ((), ())), preferred_element_type=jnp.float32)


def to_columns(kern, a_scores):
    return jnp.dot(a_scores, kern, preferred_element_type=jnp.float32)


def pairs_body(tiles, outs, *refs):
    blocks, totals = refs[:len(refs) - len(outs)], refs[len(refs) - len(outs):]
    used = sorted({t for tile in tiles for t in tile})
    norms = {t: norms_of(blocks[t]) for t in used}
    scores = {t: scores_of(blocks[t]) for t in used}
    sums = {}

    def add(t, value):
        sums[t] = value if t not in sums else sums[t] + value

    for a, b in tiles:
        kern = tile_of(blocks[a], norms[a][0], blocks[b], norms[b][1])
        add(a, to_rows(kern, scores[b]))
        if a != b:
            add(b, to_columns(kern, scores[a]))
    for t, total in zip(outs, totals):
        total[...] = sums[t]


VMEM = pl.BlockSpec(memory_space=pltpu.VMEM)


def cost(tiles, blocks):
    return pl.CostEstimate(
        flops=tiles * 2 * BLK * BLK * (WAVE + 2 * COLS),
        bytes_accessed=blocks * (BLK + PACK) * WAVE * 2,
        transcendentals=tiles * BLK * BLK,
    )


def last_body(zero_ref, down_ref, down2_ref, extra_ref, zero_in, nine_in, eight_in, two_in, *totals):
    zero_total, nine_total, eight_total, extra_total, two_total = totals
    column, _ = norms_of(extra_ref)
    extra_scores = scores_of(extra_ref)
    sums = None
    for ref, before, after in (
        (zero_ref, zero_in, zero_total), (down_ref, nine_in, nine_total), (down2_ref, eight_in, eight_total)
    ):
        kern = tile_of(extra_ref, column, ref, norms_of(ref)[1])
        mine = to_rows(kern, scores_of(ref))
        sums = mine if sums is None else sums + mine
        after[...] = before[...] + to_columns(kern, extra_scores)
    extra_total[...] = sums
    two_total[...] = two_in[...]


def last_pairs(blocks, sums):
    return pl.pallas_call(
        last_body,
        out_shape=[jax.ShapeDtypeStruct((COLS, BLK), jnp.float32)] * 5,
        in_specs=[VMEM] * 8,
        out_specs=[VMEM] * 5,
        compiler_params=pltpu.CompilerParams(vmem_limit_bytes=12 * 1024 * 1024),
        cost_estimate=cost(3, 4),
    )(*blocks, *sums)


def pairs(blocks, tiles, outs):
    return pl.pallas_call(
        functools.partial(pairs_body, tiles, outs),
        out_shape=[jax.ShapeDtypeStruct((COLS, BLK), jnp.float32)] * len(outs),
        in_specs=[VMEM] * len(blocks),
        out_specs=[VMEM] * len(outs),
        compiler_params=pltpu.CompilerParams(vmem_limit_bytes=12 * 1024 * 1024),
        cost_estimate=cost(len(tiles), len(blocks)),
    )(*blocks)


def sibling_body(kind_ref, extra_ref, zero_ref, up_ref, down_ref, up2_ref, down2_ref, *totals):
    extra_total, zero_total, up_total, down_total, up2_total, down2_total = totals
    column, _ = norms_of(extra_ref)
    extra_scores = scores_of(extra_ref)

    def one(ref):
        kern = tile_of(extra_ref, column, ref, norms_of(ref)[1])
        return to_rows(kern, scores_of(ref)), to_columns(kern, extra_scores)

    total, zero_total[...] = one(zero_ref)
    mine, up_total[...] = one(up_ref)
    total = total + mine
    mine, down_total[...] = one(down_ref)
    extra_total[...] = total + mine

    @pl.when(kind_ref[0] == 0)
    def _():
        value, up2_total[...] = one(up2_ref)
        extra_total[...] += value
        down2_total[...] = jnp.zeros_like(down2_total)

    @pl.when(kind_ref[0] != 0)
    def _():
        value, down2_total[...] = one(down2_ref)
        extra_total[...] += value
        up2_total[...] = jnp.zeros_like(up2_total)


def sibling_pairs(kind, blocks):
    return pl.pallas_call(
        sibling_body,
        out_shape=[jax.ShapeDtypeStruct((COLS, BLK), jnp.float32)] * 6,
        in_specs=[pl.BlockSpec(memory_space=pltpu.SMEM)] + [VMEM] * 6,
        out_specs=[VMEM] * 6,
        compiler_params=pltpu.CompilerParams(vmem_limit_bytes=12 * 1024 * 1024),
        cost_estimate=cost(4, 6),
    )(kind, *blocks)


def on_device(spectra, scores):
    n = lax.axis_size(AXES)
    quads = n // 4
    me = lax.axis_index(AXES)
    kind = (((me >> 1) ^ me) & 1).astype(jnp.int32).reshape(1)

    column = lax.axis_size("gy") // 4
    level = (me >> 2) % column
    side = (me >> 1) & 1
    low, high = level < 2, level >= column - 2
    far_up = jnp.where(side == 0, high, low)
    far_down = jnp.where(side == 0, low, high)
    back_up = level == jnp.where(side == 0, column - 1, 0)
    back_down = level == jnp.where(side == 0, 0, column - 1)

    def route(block, source_of):
        return lax.ppermute(block, AXES, sources(source_of, n, column))

    zero = packed(spectra, scores)
    far = route(zero, far_source)
    up = route(zero, lambda i, column, quads: near_source(i, 1, 1, column, quads))
    down = route(zero, lambda i, column, quads: near_source(i, -1, 1, column, quads))
    up2 = route(up, lambda i, column, quads: near_source(i, 1, 2, column, quads))
    down2 = route(down, lambda i, column, quads: near_source(i, -1, 2, column, quads))
    edge = back_level(me, column)
    back = route(jnp.where(edge, far, jnp.where(side == 0, up, down)), back_source)
    up2 = jnp.where(far_up, far, up2)
    down2 = jnp.where(far_down, far, down2)
    back, _, _ = lax.optimization_barrier((back, up2, down2))
    up = jnp.where(back_up, back, up)
    down = jnp.where(back_down, back, down)
    sibling = fetch(up2, lambda i: i ^ 1, n)
    second = fetch(up2, lambda i: second_partner(i, quads), n)
    first = fetch(jnp.where(me < n, down, up2), lambda i: first_partner(i, quads), n)

    a0, a1, a9 = pairs([zero, up, down], ((0, 0), (0, 1), (2, 1)), (0, 1, 2))
    b0, b1, b9, b2, b8, bs = pairs(
        [zero, up, down, up2, down2, second],
        ((2, 3), (4, 3), (5, 0), (5, 1), (5, 2), (5, 3), (5, 4)),
        (0, 1, 2, 3, 4, 5),
    )
    df, d0, d1, d9, d2, d8 = sibling_pairs(kind, [sibling, zero, up, down, up2, down2])
    def send(block, source_of):
        pairs_of = sources(source_of, n, column)
        return lax.ppermute(block, AXES, [(i, source) for source, i in pairs_of])

    none = jnp.zeros_like(a0)
    one = a1 + b1 + d1
    two = b2 + d2 + give(df, lambda i: i ^ 1, n)
    total, nine, eight, cf, two = last_pairs(
        [zero, down, down2, first], [a0 + b0 + d0, a9 + b9 + d9, b8 + d8, two]
    )
    two = two + give(bs, lambda i: second_partner(i, quads), n)
    nine = nine + give(cf, lambda i: first_partner(i, quads), n)
    total = total + send(two, lambda i, column, quads: inner_source(i, 2, column, quads))
    total = total + send(eight, lambda i, column, quads: inner_source(i, -2, column, quads))
    upward = send(
        jnp.concatenate([one, jnp.where(back_down, nine, none)]),
        lambda i, column, quads: near_source(i, 1, 1, column, quads),
    )
    downward = send(
        jnp.concatenate([nine, jnp.where(back_up, one, none)]),
        lambda i, column, quads: near_source(i, -1, 1, column, quads),
    )
    total = total + upward[:COLS] + downward[:COLS]
    crossing = jnp.where(far_up, two + downward[COLS:], eight + upward[COLS:])
    total = total + send(crossing, far_source)
    return total.T


def solution(mesh):
    return jax.shard_map(
        on_device,
        mesh=mesh,
        in_specs=(P(AXES, None), P(AXES, None)),
        out_specs=P(AXES, None),
        check_vma=False,
    )
```

```python
import functools

import jax
import jax.numpy as jnp
from jax import lax
from jax.experimental import pallas as pl
from jax.experimental.pallas import tpu as pltpu
from jax.sharding import PartitionSpec as P

WAVE = 1024
BLK = 224
COLS = 32
PACK = 16
AXES = ("gx", "gy")

spread_rate = 4.0


def split(i):
    return i >> 2, (i >> 1) & 1, i & 1


def device(quad, side, core, quads):
    return (quad % quads) * 4 + side * 2 + core


def stepped(i, j, quads):
    quad, side, core = split(i)
    return device(quad + j, side, core, quads)


def within(i, j, column, quads):
    return stepped(i, j, quads) // (4 * column) == i // (4 * column)


def near_source(i, j, steps, column, quads):
    return stepped(i, j, quads) if within(i, j * steps, column, quads) else None


def far_source(i, column, quads):
    for j in (2, -2):
        if not within(i, j, column, quads):
            return stepped(i, j, quads)
    return None


def back_level(me, column):
    level = (me >> 2) % column
    return (level == 1) | (level == column - 2)


def back_source(i, column, quads):
    for j in (1, -1):
        if not within(i, j, column, quads):
            return stepped(i, -j, quads)
    return None


def sources(source_of, n, column):
    found = [(source_of(i, column, n // 4), i) for i in range(n)]
    return [(source, i) for source, i in found if source is not None]


def packed(spectra, scores):
    turned = scores.T
    both = jnp.concatenate(
        [jnp.pad(turned[:PACK], ((0, 0), (0, 32))), jnp.pad(turned[PACK:], ((0, 0), (0, WAVE - 256 - BLK)))], axis=1
    )
    return jnp.concatenate([spectra, both], axis=0)


def rows_of(ref):
    return ref[0:BLK, :]


def scores_of(ref):
    return jnp.concatenate([ref[BLK:BLK + PACK, 0:BLK], ref[BLK:BLK + PACK, 256:256 + BLK]], axis=0)


def norms_of(ref):
    x = rows_of(ref).astype(jnp.float32)
    column = jnp.sum(x * x, axis=1, keepdims=True)
    row = jnp.broadcast_to(column, (BLK, 128)).T[0:1, :]
    return column, row


def tile_of(a_ref, a_column, b_ref, b_row):
    cross = lax.dot_general(
        rows_of(a_ref), rows_of(b_ref), (((1,), (1,)), ((), ())), preferred_element_type=jnp.float32
    )
    dist = a_column + b_row - 2.0 * cross
    return jnp.exp(-spread_rate * dist / WAVE).astype(jnp.bfloat16)


def to_rows(kern, b_scores):
    return lax.dot_general(b_scores, kern, (((1,), (1,)), ((), ())), preferred_element_type=jnp.float32)


def to_columns(kern, a_scores):
    return jnp.dot(a_scores, kern, preferred_element_type=jnp.float32)


def pairs_body(tiles, outs, *refs):
    blocks, totals = refs[:len(refs) - len(outs)], refs[len(refs) - len(outs):]
    used = sorted({t for tile in tiles for t in tile})
    norms = {t: norms_of(blocks[t]) for t in used}
    scores = {t: scores_of(blocks[t]) for t in used}
    sums = {}

    def add(t, value):
        sums[t] = value if t not in sums else sums[t] + value

    for a, b in tiles:
        kern = tile_of(blocks[a], norms[a][0], blocks[b], norms[b][1])
        add(a, to_rows(kern, scores[b]))
        if a != b:
            add(b, to_columns(kern, scores[a]))
    for t, total in zip(outs, totals):
        total[...] = sums[t]


VMEM = pl.BlockSpec(memory_space=pltpu.VMEM)


def cost(tiles, blocks):
    return pl.CostEstimate(
        flops=tiles * 2 * BLK * BLK * (WAVE + 2 * COLS),
        bytes_accessed=blocks * (BLK + PACK) * WAVE * 2,
        transcendentals=tiles * BLK * BLK,
    )


def pairs(blocks, tiles, outs):
    return pl.pallas_call(
        functools.partial(pairs_body, tiles, outs),
        out_shape=[jax.ShapeDtypeStruct((COLS, BLK), jnp.float32)] * len(outs),
        in_specs=[VMEM] * len(blocks),
        out_specs=[VMEM] * len(outs),
        compiler_params=pltpu.CompilerParams(vmem_limit_bytes=24 * 1024 * 1024),
        cost_estimate=cost(len(tiles), len(blocks)),
    )(*blocks)


def extras_body(
    rank_ref, extra_ref, zero_ref, up_ref, down_ref, up2_ref, down2_ref,
    zero_in, up_in, down_in, up2_in, down2_in,
    zero_total, up_total, down_total, down2_total, quad_total,
):
    rank = rank_ref[0]
    zero_total[...] = zero_in[...]
    up_total[...] = up_in[...]
    down_total[...] = down_in[...]
    down2_total[...] = down2_in[...]
    quad_total[rank] = up2_in[...]

    def one_partner(step, carry):
        other = (rank + step) & 3
        extra = extra_ref.at[other]
        column, _ = norms_of(extra)
        extra_scores = scores_of(extra)

        def one(ref):
            kern = tile_of(extra, column, ref, norms_of(ref)[1])
            return to_rows(kern, scores_of(ref)), to_columns(kern, extra_scores)

        mine, theirs = one(zero_ref)
        zero_total[...] += theirs
        more, theirs = one(up_ref)
        up_total[...] += theirs
        mine = mine + more
        more, theirs = one(down_ref)
        down_total[...] += theirs
        quad_total[other] = mine + more

        @pl.when(other > rank)
        def _():
            more, theirs = one(up2_ref)
            quad_total[rank] += theirs
            quad_total[other] += more

        @pl.when(other < rank)
        def _():
            more, theirs = one(down2_ref)
            down2_total[...] += theirs
            quad_total[other] += more

        return carry

    lax.fori_loop(1, 4, one_partner, 0)


def extras(rank, gathered, blocks, sums):
    total = jax.ShapeDtypeStruct((COLS, BLK), jnp.float32)
    return pl.pallas_call(
        extras_body,
        out_shape=[total] * 4 + [jax.ShapeDtypeStruct((4, COLS, BLK), jnp.float32)],
        in_specs=[pl.BlockSpec(memory_space=pltpu.SMEM)] + [VMEM] * 11,
        out_specs=[VMEM] * 5,
        compiler_params=pltpu.CompilerParams(vmem_limit_bytes=16 * 1024 * 1024),
        cost_estimate=cost(12, 9),
    )(rank, gathered, *blocks, *sums)


def on_device(spectra, scores):
    n = lax.axis_size(AXES)
    quads = n // 4
    me = lax.axis_index(AXES)
    column = lax.axis_size("gy") // 4
    level = (me >> 2) % column
    low, high = level < 2, level >= column - 2
    groups = [[4 * quad + rank for rank in range(4)] for quad in range(column)]

    def route(block, source_of):
        return lax.ppermute(block, AXES, sources(source_of, n, column))

    def give(block, j):
        return lax.ppermute(block, AXES, [(i, stepped(i, j, quads)) for i in range(n)])

    zero = packed(spectra, scores)
    far = route(zero, far_source)
    up = route(zero, lambda i, column, quads: near_source(i, 1, 1, column, quads))
    down = route(zero, lambda i, column, quads: near_source(i, -1, 1, column, quads))
    up2 = route(up, lambda i, column, quads: near_source(i, 1, 2, column, quads))
    down2 = route(down, lambda i, column, quads: near_source(i, -1, 2, column, quads))
    back = route(jnp.where(back_level(me, column), far, jnp.where(high, up, down)), back_source)
    up2 = jnp.where(high, far, up2)
    gathered = lax.all_gather(up2, "gy", axis_index_groups=groups)
    down2 = jnp.where(low, far, down2)
    back, _, _ = lax.optimization_barrier((back, up2, down2))
    up = jnp.where(level == column - 1, back, up)
    down = jnp.where(level == 0, back, down)

    a0, a1, a9, a2, a8 = pairs(
        [zero, up, down, up2, down2], ((0, 0), (0, 1), (2, 1), (2, 3), (4, 3)), (0, 1, 2, 3, 4)
    )
    e0, e1, e9, e8, quad = extras(
        (me & 3).astype(jnp.int32).reshape(1), gathered, [zero, up, down, up2, down2], [a0, a1, a9, a2, a8]
    )
    e2 = lax.psum_scatter(quad, "gy", scatter_dimension=0, axis_index_groups=groups)
    total = e0 + give(e1, 1) + give(e9, -1) + give(e8, -2) + give(e2, 2)
    return total.T


def solution(mesh):
    return jax.shard_map(
        on_device,
        mesh=mesh,
        in_specs=(P(AXES, None), P(AXES, None)),
        out_specs=P(AXES, None),
        check_vma=False,
    )
```

```python
import functools

import jax
import jax.numpy as jnp
from jax import lax
from jax.experimental import pallas as pl
from jax.experimental.pallas import tpu as pltpu
from jax.sharding import PartitionSpec as P

WAVE = 1024
BLK = 224
COLS = 32
PACK = 16
AXES = ("gx", "gy")

spread_rate = 4.0


def split(i):
    return i >> 2, (i >> 1) & 1, i & 1


def device(quad, side, core, quads):
    return (quad % quads) * 4 + side * 2 + core


def stepped(i, j, quads):
    quad, side, core = split(i)
    return device(quad + j, side, core, quads)


def within(i, j, column, quads):
    return stepped(i, j, quads) // (4 * column) == i // (4 * column)


def near_source(i, j, steps, column, quads):
    return stepped(i, j, quads) if within(i, j * steps, column, quads) else None


def inner_source(i, j, column, quads):
    return stepped(i, j, quads) if within(i, j, column, quads) else None


def far_source(i, column, quads):
    for j in (2, -2):
        if not within(i, j, column, quads):
            return stepped(i, j, quads)
    return None


def back_level(me, column):
    level = (me >> 2) % column
    return (level == 1) | (level == column - 2)


def back_source(i, column, quads):
    for j in (1, -1):
        if not within(i, j, column, quads):
            return stepped(i, -j, quads)
    return None


def sources(source_of, n, column):
    found = [(source_of(i, column, n // 4), i) for i in range(n)]
    return [(source, i) for source, i in found if source is not None]


def packed(spectra, scores):
    turned = scores.T
    both = jnp.concatenate(
        [jnp.pad(turned[:PACK], ((0, 0), (0, 32))), jnp.pad(turned[PACK:], ((0, 0), (0, WAVE - 256 - BLK)))], axis=1
    )
    return jnp.concatenate([spectra, both], axis=0)


def rows_of(ref):
    return ref[0:BLK, :]


def scores_of(ref):
    return jnp.concatenate([ref[BLK:BLK + PACK, 0:BLK], ref[BLK:BLK + PACK, 256:256 + BLK]], axis=0)


def norms_of(ref):
    x = rows_of(ref).astype(jnp.float32)
    column = jnp.sum(x * x, axis=1, keepdims=True)
    row = jnp.broadcast_to(column, (BLK, 128)).T[0:1, :]
    return column, row


def tile_of(a_ref, a_column, b_ref, b_row):
    cross = lax.dot_general(
        rows_of(a_ref), rows_of(b_ref), (((1,), (1,)), ((), ())), preferred_element_type=jnp.float32
    )
    dist = a_column + b_row - 2.0 * cross
    return jnp.exp(-spread_rate * dist / WAVE).astype(jnp.bfloat16)


def to_rows(kern, b_scores):
    return lax.dot_general(b_scores, kern, (((1,), (1,)), ((), ())), preferred_element_type=jnp.float32)


def to_columns(kern, a_scores):
    return jnp.dot(a_scores, kern, preferred_element_type=jnp.float32)


def pairs_body(tiles, outs, *refs):
    blocks, totals = refs[:len(refs) - len(outs)], refs[len(refs) - len(outs):]
    used = sorted({t for tile in tiles for t in tile})
    norms = {t: norms_of(blocks[t]) for t in used}
    scores = {t: scores_of(blocks[t]) for t in used}
    sums = {}

    def add(t, value):
        sums[t] = value if t not in sums else sums[t] + value

    for a, b in tiles:
        kern = tile_of(blocks[a], norms[a][0], blocks[b], norms[b][1])
        add(a, to_rows(kern, scores[b]))
        if a != b:
            add(b, to_columns(kern, scores[a]))
    for t, total in zip(outs, totals):
        total[...] = sums[t]


VMEM = pl.BlockSpec(memory_space=pltpu.VMEM)


def cost(tiles, blocks):
    return pl.CostEstimate(
        flops=tiles * 2 * BLK * BLK * (WAVE + 2 * COLS),
        bytes_accessed=blocks * (BLK + PACK) * WAVE * 2,
        transcendentals=tiles * BLK * BLK,
    )


def pairs(blocks, tiles, outs):
    return pl.pallas_call(
        functools.partial(pairs_body, tiles, outs),
        out_shape=[jax.ShapeDtypeStruct((COLS, BLK), jnp.float32)] * len(outs),
        in_specs=[VMEM] * len(blocks),
        out_specs=[VMEM] * len(outs),
        compiler_params=pltpu.CompilerParams(vmem_limit_bytes=12 * 1024 * 1024),
        cost_estimate=cost(len(tiles), len(blocks)),
    )(*blocks)


def extra_body(
    low_ref, extra_ref, zero_ref, up_ref, down_ref, up2_ref, down2_ref,
    zero_in, up_in, down_in, up2_in, down2_in,
    zero_total, up_total, down_total, up2_total, down2_total, extra_total,
):
    column, _ = norms_of(extra_ref)
    extra_scores = scores_of(extra_ref)

    def one(ref, before, after):
        kern = tile_of(extra_ref, column, ref, norms_of(ref)[1])
        after[...] = before[...] + to_columns(kern, extra_scores)
        return to_rows(kern, scores_of(ref))

    mine = one(zero_ref, zero_in, zero_total)
    mine = mine + one(up_ref, up_in, up_total)
    extra_total[...] = mine + one(down_ref, down_in, down_total)

    @pl.when(low_ref[0] != 0)
    def _():
        extra_total[...] += one(up2_ref, up2_in, up2_total)
        down2_total[...] = down2_in[...]

    @pl.when(low_ref[0] == 0)
    def _():
        extra_total[...] += one(down2_ref, down2_in, down2_total)
        up2_total[...] = up2_in[...]


def extra_pairs(is_low, extra, blocks, sums):
    total = jax.ShapeDtypeStruct((COLS, BLK), jnp.float32)
    outs = pl.pallas_call(
        extra_body,
        out_shape=[total] * 6,
        in_specs=[pl.BlockSpec(memory_space=pltpu.SMEM)] + [VMEM] * 11,
        out_specs=[VMEM] * 6,
        compiler_params=pltpu.CompilerParams(vmem_limit_bytes=12 * 1024 * 1024),
        cost_estimate=cost(4, 6),
    )(is_low.astype(jnp.int32).reshape(1), extra, *blocks, *sums)
    return outs[:5], outs[5]


def on_device(spectra, scores):
    n = lax.axis_size(AXES)
    quads = n // 4
    me = lax.axis_index(AXES)
    column = lax.axis_size("gy") // 4
    level = (me >> 2) % column
    low, high = level < 2, level >= column - 2
    def route(block, source_of):
        return lax.ppermute(block, AXES, sources(source_of, n, column))

    def send(block, source_of):
        return lax.ppermute(block, AXES, [(i, source) for source, i in sources(source_of, n, column)])

    def swap(block, bits):
        return lax.ppermute(block, AXES, [(i, i ^ bits) for i in range(n)])

    zero = packed(spectra, scores)
    far = route(zero, far_source)
    up = route(zero, lambda i, column, quads: near_source(i, 1, 1, column, quads))
    down = route(zero, lambda i, column, quads: near_source(i, -1, 1, column, quads))
    up2 = route(up, lambda i, column, quads: near_source(i, 1, 2, column, quads))
    late = jnp.where(me < n, down, jnp.where(high, far, up2))
    down2 = route(late, lambda i, column, quads: near_source(i, -1, 2, column, quads))
    back = route(jnp.where(back_level(me, column), far, jnp.where(high, up, down)), back_source)
    up2 = jnp.where(high, far, up2)
    sibling, beside, across = swap(up2, 1), swap(up2, 2), swap(up2, 3)
    down2 = jnp.where(low, far, down2)
    back, _, _ = lax.optimization_barrier((back, up2, down2))
    up = jnp.where(level == column - 1, back, up)
    down = jnp.where(level == 0, back, down)

    blocks = [zero, up, down, up2, down2]
    sums = pairs(blocks, ((0, 0), (0, 1), (2, 1), (2, 3), (4, 3)), (0, 1, 2, 3, 4))
    sums, for_sibling = extra_pairs((me & 1) == 0, sibling, blocks, sums)
    sums, for_beside = extra_pairs((me & 2) == 0, beside, blocks, sums)
    sums, for_across = extra_pairs((me & 2) == 0, across, blocks, sums)
    total, one, nine, two, eight = sums
    two = two + swap(for_sibling, 1) + swap(for_beside, 2) + swap(for_across, 3)

    none = jnp.zeros_like(one)
    upward = send(
        jnp.concatenate([one, jnp.where(level == 0, nine, none)]),
        lambda i, column, quads: near_source(i, 1, 1, column, quads),
    )
    downward = send(
        jnp.concatenate([nine, jnp.where(level == column - 1, one, none)]),
        lambda i, column, quads: near_source(i, -1, 1, column, quads),
    )
    total = total + upward[:COLS] + downward[:COLS]
    crossing = jnp.where(high, two + downward[COLS:], eight + upward[COLS:])
    total = total + send(crossing, far_source)
    total = total + send(two, lambda i, column, quads: inner_source(i, 2, column, quads))
    total = total + send(eight, lambda i, column, quads: inner_source(i, -2, column, quads))
    return total.T


def solution(mesh):
    return jax.shard_map(
        on_device,
        mesh=mesh,
        in_specs=(P(AXES, None), P(AXES, None)),
        out_specs=P(AXES, None),
        check_vma=False,
    )
```

```python
import functools

import jax
import jax.numpy as jnp
from jax import lax
from jax.experimental import pallas as pl
from jax.experimental.pallas import tpu as pltpu
from jax.sharding import PartitionSpec as P

WAVE = 1024
BLK = 224
COLS = 32
PACK = 16
AXES = ("gx", "gy")

spread_rate = 4.0


def split(i):
    return i >> 2, (i >> 1) & 1, i & 1


def device(quad, side, core, quads):
    return (quad % quads) * 4 + side * 2 + core


def stepped(i, j, quads):
    quad, side, core = split(i)
    return device(quad + j, side, core, quads)


def within(i, j, column, quads):
    return stepped(i, j, quads) // (4 * column) == i // (4 * column)


def near_source(i, j, steps, column, quads):
    return stepped(i, j, quads) if within(i, j * steps, column, quads) else None


def inner_source(i, j, column, quads):
    return stepped(i, j, quads) if within(i, j, column, quads) else None


def far_source(i, column, quads):
    for j in (2, -2):
        if not within(i, j, column, quads):
            return stepped(i, j, quads)
    return None


def back_level(me, column):
    level = (me >> 2) % column
    return (level == 1) | (level == column - 2)


def back_source(i, column, quads):
    for j in (1, -1):
        if not within(i, j, column, quads):
            return stepped(i, -j, quads)
    return None


def sources(source_of, n, column):
    found = [(source_of(i, column, n // 4), i) for i in range(n)]
    return [(source, i) for source, i in found if source is not None]


VMEM = pl.BlockSpec(memory_space=pltpu.VMEM)


def packed_body(spectra_ref, scores_ref, out_ref):
    out_ref[0:BLK, :] = spectra_ref[...]
    turned = scores_ref[...].astype(jnp.float32).T.astype(jnp.bfloat16)
    out_ref[BLK:BLK + PACK, :] = jnp.zeros((PACK, WAVE), jnp.bfloat16)
    out_ref[BLK:BLK + PACK, 0:BLK] = turned[0:PACK]
    out_ref[BLK:BLK + PACK, 256:256 + BLK] = turned[PACK:COLS]


def packed(spectra, scores):
    return pl.pallas_call(
        packed_body,
        out_shape=jax.ShapeDtypeStruct((BLK + PACK, WAVE), jnp.bfloat16),
        in_specs=[VMEM] * 2,
        out_specs=VMEM,
        compiler_params=pltpu.CompilerParams(vmem_limit_bytes=12 * 1024 * 1024),
        cost_estimate=pl.CostEstimate(flops=0, bytes_accessed=4 * BLK * WAVE, transcendentals=0),
    )(spectra, scores)


def rows_of(ref):
    return ref[0:BLK, :]


def scores_of(ref):
    return jnp.concatenate([ref[BLK:BLK + PACK, 0:BLK], ref[BLK:BLK + PACK, 256:256 + BLK]], axis=0)


def norms_of(ref):
    x = rows_of(ref).astype(jnp.float32)
    column = jnp.sum(x * x, axis=1, keepdims=True)
    row = jnp.broadcast_to(column, (BLK, 128)).T[0:1, :]
    return column, row


def tile_of(a_ref, a_column, b_ref, b_row):
    cross = lax.dot_general(
        rows_of(a_ref), rows_of(b_ref), (((1,), (1,)), ((), ())), preferred_element_type=jnp.float32
    )
    dist = a_column + b_row - 2.0 * cross
    return jnp.exp(-spread_rate * dist / WAVE).astype(jnp.bfloat16)


def to_rows(kern, b_scores):
    return lax.dot_general(b_scores, kern, (((1,), (1,)), ((), ())), preferred_element_type=jnp.float32)


def to_columns(kern, a_scores):
    return jnp.dot(a_scores, kern, preferred_element_type=jnp.float32)


def pairs_body(tiles, outs, *refs):
    blocks, totals = refs[:len(refs) - len(outs)], refs[len(refs) - len(outs):]
    used = sorted({t for tile in tiles for t in tile})
    norms = {t: norms_of(blocks[t]) for t in used}
    scores = {t: scores_of(blocks[t]) for t in used}
    sums = {}

    def add(t, value):
        sums[t] = value if t not in sums else sums[t] + value

    for a, b in tiles:
        kern = tile_of(blocks[a], norms[a][0], blocks[b], norms[b][1])
        add(a, to_rows(kern, scores[b]))
        if a != b:
            add(b, to_columns(kern, scores[a]))
    for t, total in zip(outs, totals):
        total[...] = sums[t]


def cost(tiles, blocks):
    return pl.CostEstimate(
        flops=tiles * 2 * BLK * BLK * (WAVE + 2 * COLS),
        bytes_accessed=blocks * (BLK + PACK) * WAVE * 2,
        transcendentals=tiles * BLK * BLK,
    )


def pairs(blocks, tiles, outs):
    return pl.pallas_call(
        functools.partial(pairs_body, tiles, outs),
        out_shape=[jax.ShapeDtypeStruct((COLS, BLK), jnp.float32)] * len(outs),
        in_specs=[VMEM] * len(blocks),
        out_specs=[VMEM] * len(outs),
        compiler_params=pltpu.CompilerParams(vmem_limit_bytes=12 * 1024 * 1024),
        cost_estimate=cost(len(tiles), len(blocks)),
    )(*blocks)


def extra_body(
    low_ref, extra_ref, zero_ref, up_ref, down_ref, up2_ref, down2_ref,
    zero_in, up_in, down_in, up2_in, down2_in,
    zero_total, up_total, down_total, up2_total, down2_total, extra_total,
):
    column, _ = norms_of(extra_ref)
    extra_scores = scores_of(extra_ref)

    def one(ref, before, after):
        kern = tile_of(extra_ref, column, ref, norms_of(ref)[1])
        after[...] = before[...] + to_columns(kern, extra_scores)
        return to_rows(kern, scores_of(ref))

    mine = one(zero_ref, zero_in, zero_total)
    mine = mine + one(up_ref, up_in, up_total)
    extra_total[...] = mine + one(down_ref, down_in, down_total)

    @pl.when(low_ref[0] != 0)
    def _():
        extra_total[...] += one(up2_ref, up2_in, up2_total)
        down2_total[...] = down2_in[...]

    @pl.when(low_ref[0] == 0)
    def _():
        extra_total[...] += one(down2_ref, down2_in, down2_total)
        up2_total[...] = up2_in[...]


def extra_pairs(is_low, extra, blocks, sums):
    total = jax.ShapeDtypeStruct((COLS, BLK), jnp.float32)
    outs = pl.pallas_call(
        extra_body,
        out_shape=[total] * 6,
        in_specs=[pl.BlockSpec(memory_space=pltpu.SMEM)] + [VMEM] * 11,
        out_specs=[VMEM] * 6,
        compiler_params=pltpu.CompilerParams(vmem_limit_bytes=12 * 1024 * 1024),
        cost_estimate=cost(4, 6),
    )(is_low.astype(jnp.int32).reshape(1), extra, *blocks, *sums)
    return outs[:5], outs[5]


def on_device(spectra, scores):
    n = lax.axis_size(AXES)
    quads = n // 4
    me = lax.axis_index(AXES)
    column = lax.axis_size("gy") // 4
    level = (me >> 2) % column
    low, high = level < 2, level >= column - 2
    def route(block, source_of):
        return lax.ppermute(block, AXES, sources(source_of, n, column))

    def send(block, source_of):
        return lax.ppermute(block, AXES, [(i, source) for source, i in sources(source_of, n, column)])

    def swap(block, bits):
        return lax.ppermute(block, AXES, [(i, i ^ bits) for i in range(n)])

    zero = packed(spectra, scores)
    far = route(zero, far_source)
    up = route(zero, lambda i, column, quads: near_source(i, 1, 1, column, quads))
    down = route(zero, lambda i, column, quads: near_source(i, -1, 1, column, quads))
    up2 = route(up, lambda i, column, quads: near_source(i, 1, 2, column, quads))
    down2 = route(down, lambda i, column, quads: near_source(i, -1, 2, column, quads))
    back = route(jnp.where(back_level(me, column), far, up2), back_source)
    up2 = jnp.where(high, far, up2)
    beside = swap(up2, 2)
    sibling = swap(up2, 1)
    across = swap(beside, 1)
    down2 = jnp.where(low, far, down2)
    back, _, _ = lax.optimization_barrier((back, up2, down2))
    up = jnp.where(level == column - 1, back, up)
    down = jnp.where(level == 0, back, down)

    blocks = [zero, up, down, up2, down2]
    sums = pairs(blocks, ((0, 0), (0, 1), (2, 1), (2, 3), (4, 3)), (0, 1, 2, 3, 4))
    sums, for_sibling = extra_pairs((me & 1) == 0, sibling, blocks, sums)
    sums, for_beside = extra_pairs((me & 2) == 0, beside, blocks, sums)
    total, one, nine, two, eight = sums
    two = two + swap(for_sibling, 1) + swap(for_beside, 2)
    sums, for_across = extra_pairs((me & 2) == 0, across, blocks, [total, one, nine, two, eight])
    total, one, nine, two, eight = sums
    two = two + swap(for_across, 3)

    none = jnp.zeros_like(one)
    upward = send(
        jnp.concatenate([one, jnp.where(level == 0, nine, none)]),
        lambda i, column, quads: near_source(i, 1, 1, column, quads),
    )
    downward = send(
        jnp.concatenate([nine, jnp.where(level == column - 1, one, none)]),
        lambda i, column, quads: near_source(i, -1, 1, column, quads),
    )
    total = total + upward[:COLS] + downward[:COLS]
    crossing = jnp.where(high, two + downward[COLS:], eight + upward[COLS:])
    total = total + send(crossing, far_source)
    total = total + send(two, lambda i, column, quads: inner_source(i, 2, column, quads))
    eight = jnp.where(me < n, eight, crossing)
    total = total + send(eight, lambda i, column, quads: inner_source(i, -2, column, quads))
    return total.T


def solution(mesh):
    return jax.shard_map(
        on_device,
        mesh=mesh,
        in_specs=(P(AXES, None), P(AXES, None)),
        out_specs=P(AXES, None),
        check_vma=False,
    )
```

```python
import functools

import jax
import jax.numpy as jnp
from jax import lax
from jax.experimental import pallas as pl
from jax.experimental.pallas import tpu as pltpu
from jax.sharding import PartitionSpec as P

WAVE = 1024
BLK = 224
COLS = 32
PACK = 16
AXES = ("gx", "gy")

spread_rate = 4.0


def split(i):
    return i >> 2, (i >> 1) & 1, i & 1


def device(quad, side, core, quads):
    return (quad % quads) * 4 + side * 2 + core


def stepped(i, j, quads):
    quad, side, core = split(i)
    return device(quad + j, side, core, quads)


def within(i, j, column, quads):
    return stepped(i, j, quads) // (4 * column) == i // (4 * column)


def near_source(i, j, steps, column, quads):
    return stepped(i, j, quads) if within(i, j * steps, column, quads) else None


def far_source(i, column, quads):
    for j in (2, -2):
        if not within(i, j, column, quads):
            return stepped(i, j, quads)
    return None


def back_level(me, column):
    level = (me >> 2) % column
    return (level == 1) | (level == column - 2)


def back_source(i, column, quads):
    for j in (1, -1):
        if not within(i, j, column, quads):
            return stepped(i, -j, quads)
    return None


def sources(source_of, n, column):
    found = [(source_of(i, column, n // 4), i) for i in range(n)]
    return [(source, i) for source, i in found if source is not None]


VMEM = pl.BlockSpec(memory_space=pltpu.VMEM)


def packed_body(spectra_ref, scores_ref, out_ref):
    out_ref[0:BLK, :] = spectra_ref[...]
    turned = scores_ref[...].astype(jnp.float32).T.astype(jnp.bfloat16)
    out_ref[BLK:BLK + PACK, :] = jnp.zeros((PACK, WAVE), jnp.bfloat16)
    out_ref[BLK:BLK + PACK, 0:BLK] = turned[0:PACK]
    out_ref[BLK:BLK + PACK, 256:256 + BLK] = turned[PACK:COLS]


def packed(spectra, scores):
    return pl.pallas_call(
        packed_body,
        out_shape=jax.ShapeDtypeStruct((BLK + PACK, WAVE), jnp.bfloat16),
        in_specs=[VMEM] * 2,
        out_specs=VMEM,
        compiler_params=pltpu.CompilerParams(vmem_limit_bytes=12 * 1024 * 1024),
        cost_estimate=pl.CostEstimate(flops=0, bytes_accessed=4 * BLK * WAVE, transcendentals=0),
    )(spectra, scores)


def rows_of(ref):
    return ref[0:BLK, :]


def scores_of(ref):
    return jnp.concatenate([ref[BLK:BLK + PACK, 0:BLK], ref[BLK:BLK + PACK, 256:256 + BLK]], axis=0)


def norms_of(ref):
    x = rows_of(ref).astype(jnp.float32)
    column = jnp.sum(x * x, axis=1, keepdims=True)
    row = jnp.broadcast_to(column, (BLK, 128)).T[0:1, :]
    return column, row


def tile_of(a_ref, a_column, b_ref, b_row):
    cross = lax.dot_general(
        rows_of(a_ref), rows_of(b_ref), (((1,), (1,)), ((), ())), preferred_element_type=jnp.float32
    )
    dist = a_column + b_row - 2.0 * cross
    return jnp.exp(-spread_rate * dist / WAVE).astype(jnp.bfloat16)


def to_rows(kern, b_scores):
    return lax.dot_general(b_scores, kern, (((1,), (1,)), ((), ())), preferred_element_type=jnp.float32)


def to_columns(kern, a_scores):
    return jnp.dot(a_scores, kern, preferred_element_type=jnp.float32)


def pairs_body(tiles, outs, known, *refs):
    count = len(refs) - len(outs) - len(known)
    blocks, before, totals = refs[:count], refs[count:count + len(known)], refs[count + len(known):]
    used = sorted({t for tile in tiles for t in tile})
    norms = {t: norms_of(blocks[t]) for t in used}
    scores = {t: scores_of(blocks[t]) for t in used}
    sums = {t: ref[...] for t, ref in zip(known, before)}

    def add(t, value):
        sums[t] = value if t not in sums else sums[t] + value

    for a, b in tiles:
        kern = tile_of(blocks[a], norms[a][0], blocks[b], norms[b][1])
        add(a, to_rows(kern, scores[b]))
        if a != b:
            add(b, to_columns(kern, scores[a]))
    for t, total in zip(outs, totals):
        total[...] = sums[t]


def cost(tiles, blocks):
    return pl.CostEstimate(
        flops=tiles * 2 * BLK * BLK * (WAVE + 2 * COLS),
        bytes_accessed=blocks * (BLK + PACK) * WAVE * 2,
        transcendentals=tiles * BLK * BLK,
    )


def pairs(blocks, tiles, outs, known, sums):
    return pl.pallas_call(
        functools.partial(pairs_body, tiles, outs, known),
        out_shape=[jax.ShapeDtypeStruct((COLS, BLK), jnp.float32)] * len(outs),
        in_specs=[VMEM] * (len(blocks) + len(sums)),
        out_specs=[VMEM] * len(outs),
        compiler_params=pltpu.CompilerParams(vmem_limit_bytes=12 * 1024 * 1024),
        cost_estimate=cost(len(tiles), len(blocks)),
    )(*blocks, *sums)


def extra_body(
    low_ref, extra_ref, zero_ref, up_ref, down_ref, up2_ref, down2_ref,
    zero_in, up_in, down_in, up2_in, down2_in,
    zero_total, up_total, down_total, up2_total, down2_total, extra_total,
):
    column, _ = norms_of(extra_ref)
    extra_scores = scores_of(extra_ref)

    def one(ref, before, after):
        kern = tile_of(extra_ref, column, ref, norms_of(ref)[1])
        after[...] = before[...] + to_columns(kern, extra_scores)
        return to_rows(kern, scores_of(ref))

    mine = one(zero_ref, zero_in, zero_total)
    mine = mine + one(up_ref, up_in, up_total)
    extra_total[...] = mine + one(down_ref, down_in, down_total)

    @pl.when(low_ref[0] != 0)
    def _():
        extra_total[...] += one(up2_ref, up2_in, up2_total)
        down2_total[...] = down2_in[...]

    @pl.when(low_ref[0] == 0)
    def _():
        extra_total[...] += one(down2_ref, down2_in, down2_total)
        up2_total[...] = up2_in[...]


def extra_pairs(is_low, extra, blocks, sums):
    total = jax.ShapeDtypeStruct((COLS, BLK), jnp.float32)
    outs = pl.pallas_call(
        extra_body,
        out_shape=[total] * 6,
        in_specs=[pl.BlockSpec(memory_space=pltpu.SMEM)] + [VMEM] * 11,
        out_specs=[VMEM] * 6,
        compiler_params=pltpu.CompilerParams(vmem_limit_bytes=12 * 1024 * 1024),
        cost_estimate=cost(4, 6),
    )(is_low.astype(jnp.int32).reshape(1), extra, *blocks, *sums)
    return outs[:5], outs[5]


def early_body(low_ref, sibling_ref, beside_ref, zero_ref, up2_ref, down2_ref,
               zero_total, up2_total, down2_total, sibling_total, beside_total, chosen_ref):
    zero_column, zero_row = norms_of(zero_ref)
    zero_scores = scores_of(zero_ref)
    total = to_rows(tile_of(zero_ref, zero_column, zero_ref, zero_row), zero_scores)
    kern = tile_of(down2_ref, norms_of(down2_ref)[0], up2_ref, norms_of(up2_ref)[1])
    down2_sum = to_rows(kern, scores_of(up2_ref))
    up2_sum = to_columns(kern, scores_of(down2_ref))
    for place, (ref, extra_total) in enumerate(((sibling_ref, sibling_total), (beside_ref, beside_total))):
        low = low_ref[place] != 0
        chosen = chosen_ref.at[place]

        @pl.when(low)
        def _():
            chosen[...] = up2_ref[...]

        @pl.when(jnp.logical_not(low))
        def _():
            chosen[...] = down2_ref[...]

        column, _ = norms_of(ref)
        scores = scores_of(ref)
        kern = tile_of(ref, column, zero_ref, zero_row)
        mine = to_rows(kern, zero_scores)
        total = total + to_columns(kern, scores)
        kern = tile_of(ref, column, chosen, norms_of(chosen)[1])
        extra_total[...] = mine + to_rows(kern, scores_of(chosen))
        theirs = to_columns(kern, scores)
        up2_sum = up2_sum + jnp.where(low, theirs, 0.0)
        down2_sum = down2_sum + jnp.where(low, 0.0, theirs)
    zero_total[...] = total
    up2_total[...] = up2_sum
    down2_total[...] = down2_sum


def early_pairs(lows, blocks):
    return pl.pallas_call(
        early_body,
        out_shape=[jax.ShapeDtypeStruct((COLS, BLK), jnp.float32)] * 5,
        in_specs=[pl.BlockSpec(memory_space=pltpu.SMEM)] + [VMEM] * 5,
        out_specs=[VMEM] * 5,
        scratch_shapes=[pltpu.VMEM((2, BLK + PACK, WAVE), jnp.bfloat16)],
        compiler_params=pltpu.CompilerParams(vmem_limit_bytes=12 * 1024 * 1024),
        cost_estimate=cost(6, 5),
    )(lows, *blocks)


def on_device(spectra, scores):
    n = lax.axis_size(AXES)
    quads = n // 4
    me = lax.axis_index(AXES)
    column = lax.axis_size("gy") // 4
    level = (me >> 2) % column
    low, high = level < 2, level >= column - 2
    def route(block, source_of):
        return lax.ppermute(block, AXES, sources(source_of, n, column))

    def give(block, j):
        return lax.ppermute(block, AXES, [(i, stepped(i, j, quads)) for i in range(n)])

    def swap(block, bits):
        return lax.ppermute(block, AXES, [(i, i ^ bits) for i in range(n)])

    zero = packed(spectra, scores)
    far = route(zero, far_source)
    up = route(zero, lambda i, column, quads: near_source(i, 1, 1, column, quads))
    down = route(zero, lambda i, column, quads: near_source(i, -1, 1, column, quads))
    up2 = route(up, lambda i, column, quads: near_source(i, 1, 2, column, quads))
    down2 = route(down, lambda i, column, quads: near_source(i, -1, 2, column, quads))
    back = route(jnp.where(back_level(me, column), far, up2), back_source)
    up2 = jnp.where(high, far, up2)
    beside = swap(up2, 2)
    sibling = swap(up2, 1)
    across = swap(beside, 1)
    up2, down2 = lax.optimization_barrier((up2, down2))
    down2 = jnp.where(low, far, down2)
    back, _, _ = lax.optimization_barrier((back, up2, down2))
    up = jnp.where(level == column - 1, back, up)
    down = jnp.where(level == 0, back, down)

    lows = jnp.stack([(me & 1) == 0, (me & 2) == 0]).astype(jnp.int32)
    total, two, eight, for_sibling, for_beside = early_pairs(lows, [sibling, beside, zero, up2, down2])
    total, one, nine, two, for_sibling, for_beside = pairs(
        [zero, up, down, up2, sibling, beside],
        ((0, 1), (2, 1), (2, 3), (4, 1), (4, 2), (5, 1), (5, 2)),
        (0, 1, 2, 3, 4, 5),
        (0, 3, 4, 5),
        [total, two, for_sibling, for_beside],
    )
    two = two + swap(for_sibling, 1) + swap(for_beside, 2)
    sums, for_across = extra_pairs(
        (me & 2) == 0, across, [zero, up, down, up2, down2], [total, one, nine, two, eight]
    )
    total, one, nine, two, eight = sums
    two = two + swap(for_across, 3)
    total = total + give(one, 1) + give(nine, -1) + give(eight, -2) + give(two, 2)
    return total.T


def solution(mesh):
    return jax.shard_map(
        on_device,
        mesh=mesh,
        in_specs=(P(AXES, None), P(AXES, None)),
        out_specs=P(AXES, None),
        check_vma=False,
    )
```

```python
import functools

import jax
import jax.numpy as jnp
from jax import lax
from jax.experimental import pallas as pl
from jax.experimental.pallas import tpu as pltpu
from jax.sharding import PartitionSpec as P

WAVE = 1024
BLK = 224
COLS = 32
PACK = 16
AXES = ("gx", "gy")

spread_rate = 4.0


def split(i):
    return i >> 2, (i >> 1) & 1, i & 1


def device(quad, side, core, quads):
    return (quad % quads) * 4 + side * 2 + core


def stepped(i, j, quads):
    quad, side, core = split(i)
    return device(quad + j, side, core, quads)


def within(i, j, column, quads):
    return stepped(i, j, quads) // (4 * column) == i // (4 * column)


def near_source(i, j, steps, column, quads):
    return stepped(i, j, quads) if within(i, j * steps, column, quads) else None


def inner_source(i, j, column, quads):
    return stepped(i, j, quads) if within(i, j, column, quads) else None


def far_source(i, column, quads):
    for j in (2, -2):
        if not within(i, j, column, quads):
            return stepped(i, j, quads)
    return None


def back_level(me, column):
    level = (me >> 2) % column
    return (level == 1) | (level == column - 2)


def back_source(i, column, quads):
    for j in (1, -1):
        if not within(i, j, column, quads):
            return stepped(i, -j, quads)
    return None


def sources(source_of, n, column):
    found = [(source_of(i, column, n // 4), i) for i in range(n)]
    return [(source, i) for source, i in found if source is not None]


VMEM = pl.BlockSpec(memory_space=pltpu.VMEM)


def packed_body(spectra_ref, scores_ref, out_ref):
    out_ref[0:BLK, :] = spectra_ref[...]
    turned = scores_ref[...].astype(jnp.float32).T.astype(jnp.bfloat16)
    out_ref[BLK:BLK + PACK, :] = jnp.zeros((PACK, WAVE), jnp.bfloat16)
    out_ref[BLK:BLK + PACK, 0:BLK] = turned[0:PACK]
    out_ref[BLK:BLK + PACK, 256:256 + BLK] = turned[PACK:COLS]


def packed(spectra, scores):
    return pl.pallas_call(
        packed_body,
        out_shape=jax.ShapeDtypeStruct((BLK + PACK, WAVE), jnp.bfloat16),
        in_specs=[VMEM] * 2,
        out_specs=VMEM,
        compiler_params=pltpu.CompilerParams(vmem_limit_bytes=12 * 1024 * 1024),
        cost_estimate=pl.CostEstimate(flops=0, bytes_accessed=4 * BLK * WAVE, transcendentals=0),
    )(spectra, scores)


def rows_of(ref):
    return ref[0:BLK, :]


def scores_of(ref):
    return jnp.concatenate([ref[BLK:BLK + PACK, 0:BLK], ref[BLK:BLK + PACK, 256:256 + BLK]], axis=0)


def norms_of(ref):
    x = rows_of(ref).astype(jnp.float32)
    column = jnp.sum(x * x, axis=1, keepdims=True)
    row = jnp.broadcast_to(column, (BLK, 128)).T[0:1, :]
    return column, row


def tile_of(a_ref, a_column, b_ref, b_row):
    cross = lax.dot_general(
        rows_of(a_ref), rows_of(b_ref), (((1,), (1,)), ((), ())), preferred_element_type=jnp.float32
    )
    dist = a_column + b_row - 2.0 * cross
    return jnp.exp(-spread_rate * dist / WAVE).astype(jnp.bfloat16)


def to_rows(kern, b_scores):
    return lax.dot_general(b_scores, kern, (((1,), (1,)), ((), ())), preferred_element_type=jnp.float32)


def to_columns(kern, a_scores):
    return jnp.dot(a_scores, kern, preferred_element_type=jnp.float32)


def pairs_body(tiles, outs, known, *refs):
    count = len(refs) - len(outs) - len(known)
    blocks, before, totals = refs[:count], refs[count:count + len(known)], refs[count + len(known):]
    used = sorted({t for tile in tiles for t in tile})
    norms = {t: norms_of(blocks[t]) for t in used}
    scores = {t: scores_of(blocks[t]) for t in used}
    sums = {t: ref[...] for t, ref in zip(known, before)}

    def add(t, value):
        sums[t] = value if t not in sums else sums[t] + value

    for a, b in tiles:
        kern = tile_of(blocks[a], norms[a][0], blocks[b], norms[b][1])
        add(a, to_rows(kern, scores[b]))
        if a != b:
            add(b, to_columns(kern, scores[a]))
    for t, total in zip(outs, totals):
        total[...] = sums[t]


def cost(tiles, blocks):
    return pl.CostEstimate(
        flops=tiles * 2 * BLK * BLK * (WAVE + 2 * COLS),
        bytes_accessed=blocks * (BLK + PACK) * WAVE * 2,
        transcendentals=tiles * BLK * BLK,
    )


def pairs(blocks, tiles, outs, known, sums):
    return pl.pallas_call(
        functools.partial(pairs_body, tiles, outs, known),
        out_shape=[jax.ShapeDtypeStruct((COLS, BLK), jnp.float32)] * len(outs),
        in_specs=[VMEM] * (len(blocks) + len(sums)),
        out_specs=[VMEM] * len(outs),
        compiler_params=pltpu.CompilerParams(vmem_limit_bytes=12 * 1024 * 1024),
        cost_estimate=cost(len(tiles), len(blocks)),
    )(*blocks, *sums)


def extra_body(
    low_ref, extra_ref, zero_ref, up_ref, down_ref, up2_ref, down2_ref,
    zero_in, up_in, down_in, up2_in, down2_in,
    zero_total, up_total, down_total, up2_total, down2_total, extra_total,
):
    column, _ = norms_of(extra_ref)
    extra_scores = scores_of(extra_ref)

    def one(ref, before, after):
        kern = tile_of(extra_ref, column, ref, norms_of(ref)[1])
        after[...] = before[...] + to_columns(kern, extra_scores)
        return to_rows(kern, scores_of(ref))

    mine = one(zero_ref, zero_in, zero_total)
    mine = mine + one(up_ref, up_in, up_total)
    extra_total[...] = mine + one(down_ref, down_in, down_total)

    @pl.when(low_ref[0] != 0)
    def _():
        extra_total[...] += one(up2_ref, up2_in, up2_total)
        down2_total[...] = down2_in[...]

    @pl.when(low_ref[0] == 0)
    def _():
        extra_total[...] += one(down2_ref, down2_in, down2_total)
        up2_total[...] = up2_in[...]


def extra_pairs(is_low, extra, blocks, sums):
    total = jax.ShapeDtypeStruct((COLS, BLK), jnp.float32)
    outs = pl.pallas_call(
        extra_body,
        out_shape=[total] * 6,
        in_specs=[pl.BlockSpec(memory_space=pltpu.SMEM)] + [VMEM] * 11,
        out_specs=[VMEM] * 6,
        compiler_params=pltpu.CompilerParams(vmem_limit_bytes=12 * 1024 * 1024),
        cost_estimate=cost(4, 6),
    )(is_low.astype(jnp.int32).reshape(1), extra, *blocks, *sums)
    return outs[:5], outs[5]


def early_body(low_ref, extra_ref, zero_ref, up2_ref, down2_ref,
               zero_total, up2_total, down2_total, extra_total, chosen_ref):
    low = low_ref[0] != 0

    @pl.when(low)
    def _():
        chosen_ref[...] = up2_ref[...]

    @pl.when(jnp.logical_not(low))
    def _():
        chosen_ref[...] = down2_ref[...]

    zero_column, zero_row = norms_of(zero_ref)
    zero_scores = scores_of(zero_ref)
    total = to_rows(tile_of(zero_ref, zero_column, zero_ref, zero_row), zero_scores)
    kern = tile_of(down2_ref, norms_of(down2_ref)[0], up2_ref, norms_of(up2_ref)[1])
    down2_sum = to_rows(kern, scores_of(up2_ref))
    up2_sum = to_columns(kern, scores_of(down2_ref))
    column, _ = norms_of(extra_ref)
    scores = scores_of(extra_ref)
    kern = tile_of(extra_ref, column, zero_ref, zero_row)
    mine = to_rows(kern, zero_scores)
    zero_total[...] = total + to_columns(kern, scores)
    kern = tile_of(extra_ref, column, chosen_ref, norms_of(chosen_ref)[1])
    extra_total[...] = mine + to_rows(kern, scores_of(chosen_ref))
    theirs = to_columns(kern, scores)
    up2_total[...] = up2_sum + jnp.where(low, theirs, 0.0)
    down2_total[...] = down2_sum + jnp.where(low, 0.0, theirs)


def early_pairs(is_low, blocks):
    return pl.pallas_call(
        early_body,
        out_shape=[jax.ShapeDtypeStruct((COLS, BLK), jnp.float32)] * 4,
        in_specs=[pl.BlockSpec(memory_space=pltpu.SMEM)] + [VMEM] * 4,
        out_specs=[VMEM] * 4,
        scratch_shapes=[pltpu.VMEM((BLK + PACK, WAVE), jnp.bfloat16)],
        compiler_params=pltpu.CompilerParams(vmem_limit_bytes=12 * 1024 * 1024),
        cost_estimate=cost(4, 4),
    )(is_low.astype(jnp.int32).reshape(1), *blocks)


def on_device(spectra, scores):
    n = lax.axis_size(AXES)
    quads = n // 4
    me = lax.axis_index(AXES)
    column = lax.axis_size("gy") // 4
    level = (me >> 2) % column
    low, high = level < 2, level >= column - 2
    def route(block, source_of):
        return lax.ppermute(block, AXES, sources(source_of, n, column))

    def send(block, source_of):
        return lax.ppermute(block, AXES, [(i, source) for source, i in sources(source_of, n, column)])

    def swap(block, bits):
        return lax.ppermute(block, AXES, [(i, i ^ bits) for i in range(n)])

    zero = packed(spectra, scores)
    far = route(zero, far_source)
    up = route(zero, lambda i, column, quads: near_source(i, 1, 1, column, quads))
    down = route(zero, lambda i, column, quads: near_source(i, -1, 1, column, quads))
    up2 = route(up, lambda i, column, quads: near_source(i, 1, 2, column, quads))
    down2 = route(down, lambda i, column, quads: near_source(i, -1, 2, column, quads))
    back = route(jnp.where(back_level(me, column), far, up2), back_source)
    up2 = jnp.where(high, far, up2)
    beside = swap(up2, 2)
    sibling = swap(up2, 1)
    across = swap(beside, 1)
    up2, down2 = lax.optimization_barrier((up2, down2))
    down2 = jnp.where(low, far, down2)
    back, _, _ = lax.optimization_barrier((back, up2, down2))
    up = jnp.where(level == column - 1, back, up)
    down = jnp.where(level == 0, back, down)

    total, two, eight, for_sibling = early_pairs((me & 1) == 0, [sibling, zero, up2, down2])
    total, one, nine, two, for_sibling = pairs(
        [zero, up, down, up2, sibling],
        ((0, 1), (2, 1), (2, 3), (4, 1), (4, 2)),
        (0, 1, 2, 3, 4),
        (0, 3, 4),
        [total, two, for_sibling],
    )
    blocks = [zero, up, down, up2, down2]
    sums, for_beside = extra_pairs((me & 2) == 0, beside, blocks, [total, one, nine, two, eight])
    sums, for_across = extra_pairs((me & 2) == 0, across, blocks, sums)
    total, one, nine, two, eight = sums
    two = two + swap(for_sibling, 1) + swap(for_beside, 2) + swap(for_across, 3)

    crossing = jnp.where(high, two, eight)
    crossed = send(jnp.concatenate([crossing, jnp.where(high, one, nine)]), far_source)
    total = total + crossed[:COLS]
    far_sums = send(two, lambda i, column, quads: inner_source(i, 2, column, quads))
    far_sums = far_sums + send(eight, lambda i, column, quads: inner_source(i, -2, column, quads))
    total = total + far_sums
    nearer = jnp.where(me < n, crossed[COLS:], far_sums)
    upward = send(
        jnp.concatenate([one, nearer]), lambda i, column, quads: near_source(i, 1, 1, column, quads)
    )
    downward = send(
        jnp.concatenate([nine, nearer]), lambda i, column, quads: near_source(i, -1, 1, column, quads)
    )
    total = total + upward[:COLS] + downward[:COLS]
    total = total + jnp.where(level == column - 1, upward[COLS:], 0.0)
    total = total + jnp.where(level == 0, downward[COLS:], 0.0)
    return total.T


def solution(mesh):
    return jax.shard_map(
        on_device,
        mesh=mesh,
        in_specs=(P(AXES, None), P(AXES, None)),
        out_specs=P(AXES, None),
        check_vma=False,
    )
```

```python
import functools

import jax
import jax.numpy as jnp
from jax import lax
from jax.experimental import pallas as pl
from jax.experimental.pallas import tpu as pltpu
from jax.sharding import PartitionSpec as P

WAVE = 1024
BLK = 224
COLS = 32
PACK = 16
AXES = ("gx", "gy")

spread_rate = 4.0


def split(i):
    return i >> 2, (i >> 1) & 1, i & 1


def device(quad, side, core, quads):
    return (quad % quads) * 4 + side * 2 + core


def stepped(i, j, quads):
    quad, side, core = split(i)
    return device(quad + j, side, core, quads)


def within(i, j, column, quads):
    return stepped(i, j, quads) // (4 * column) == i // (4 * column)


def near_source(i, j, steps, column, quads):
    return stepped(i, j, quads) if within(i, j * steps, column, quads) else None


def inner_source(i, j, column, quads):
    return stepped(i, j, quads) if within(i, j, column, quads) else None


def far_source(i, column, quads):
    for j in (2, -2):
        if not within(i, j, column, quads):
            return stepped(i, j, quads)
    return None


def back_level(me, column):
    level = (me >> 2) % column
    return (level == 1) | (level == column - 2)


def back_source(i, column, quads):
    for j in (1, -1):
        if not within(i, j, column, quads):
            return stepped(i, -j, quads)
    return None


def sources(source_of, n, column):
    found = [(source_of(i, column, n // 4), i) for i in range(n)]
    return [(source, i) for source, i in found if source is not None]


VMEM = pl.BlockSpec(memory_space=pltpu.VMEM)


def packed_body(spectra_ref, scores_ref, out_ref):
    out_ref[0:BLK, :] = spectra_ref[...]
    turned = scores_ref[...].astype(jnp.float32).T.astype(jnp.bfloat16)
    out_ref[BLK:BLK + PACK, :] = jnp.zeros((PACK, WAVE), jnp.bfloat16)
    out_ref[BLK:BLK + PACK, 0:BLK] = turned[0:PACK]
    out_ref[BLK:BLK + PACK, 256:256 + BLK] = turned[PACK:COLS]


def packed(spectra, scores):
    return pl.pallas_call(
        packed_body,
        out_shape=jax.ShapeDtypeStruct((BLK + PACK, WAVE), jnp.bfloat16),
        in_specs=[VMEM] * 2,
        out_specs=VMEM,
        compiler_params=pltpu.CompilerParams(vmem_limit_bytes=12 * 1024 * 1024),
        cost_estimate=pl.CostEstimate(flops=0, bytes_accessed=4 * BLK * WAVE, transcendentals=0),
    )(spectra, scores)


def rows_of(ref):
    return ref[0:BLK, :]


def scores_of(ref):
    return jnp.concatenate([ref[BLK:BLK + PACK, 0:BLK], ref[BLK:BLK + PACK, 256:256 + BLK]], axis=0)


def norms_of(ref):
    x = rows_of(ref).astype(jnp.float32)
    column = jnp.sum(x * x, axis=1, keepdims=True)
    row = jnp.broadcast_to(column, (BLK, 128)).T[0:1, :]
    return column, row


def tile_of(a_ref, a_column, b_ref, b_row):
    cross = lax.dot_general(
        rows_of(a_ref), rows_of(b_ref), (((1,), (1,)), ((), ())), preferred_element_type=jnp.float32
    )
    dist = a_column + b_row - 2.0 * cross
    return jnp.exp(-spread_rate * dist / WAVE).astype(jnp.bfloat16)


def to_rows(kern, b_scores):
    return lax.dot_general(b_scores, kern, (((1,), (1,)), ((), ())), preferred_element_type=jnp.float32)


def to_columns(kern, a_scores):
    return jnp.dot(a_scores, kern, preferred_element_type=jnp.float32)


def pairs_body(tiles, outs, *refs):
    blocks, totals = refs[:len(refs) - len(outs)], refs[len(refs) - len(outs):]
    used = sorted({t for tile in tiles for t in tile})
    norms = {t: norms_of(blocks[t]) for t in used}
    scores = {t: scores_of(blocks[t]) for t in used}
    sums = {}

    def add(t, value):
        sums[t] = value if t not in sums else sums[t] + value

    for a, b in tiles:
        kern = tile_of(blocks[a], norms[a][0], blocks[b], norms[b][1])
        add(a, to_rows(kern, scores[b]))
        if a != b:
            add(b, to_columns(kern, scores[a]))
    for t, total in zip(outs, totals):
        total[...] = sums[t]


def cost(tiles, blocks):
    return pl.CostEstimate(
        flops=tiles * 2 * BLK * BLK * (WAVE + 2 * COLS),
        bytes_accessed=blocks * (BLK + PACK) * WAVE * 2,
        transcendentals=tiles * BLK * BLK,
    )


def pairs(blocks, tiles, outs):
    return pl.pallas_call(
        functools.partial(pairs_body, tiles, outs),
        out_shape=[jax.ShapeDtypeStruct((COLS, BLK), jnp.float32)] * len(outs),
        in_specs=[VMEM] * len(blocks),
        out_specs=[VMEM] * len(outs),
        compiler_params=pltpu.CompilerParams(vmem_limit_bytes=12 * 1024 * 1024),
        cost_estimate=cost(len(tiles), len(blocks)),
    )(*blocks)


def extra_body(
    low_ref, extra_ref, zero_ref, up_ref, down_ref, up2_ref, down2_ref,
    zero_in, up_in, down_in, up2_in, down2_in,
    zero_total, up_total, down_total, up2_total, down2_total, extra_total,
):
    column, _ = norms_of(extra_ref)
    extra_scores = scores_of(extra_ref)

    def one(ref, before, after):
        kern = tile_of(extra_ref, column, ref, norms_of(ref)[1])
        after[...] = before[...] + to_columns(kern, extra_scores)
        return to_rows(kern, scores_of(ref))

    mine = one(zero_ref, zero_in, zero_total)
    mine = mine + one(up_ref, up_in, up_total)
    extra_total[...] = mine + one(down_ref, down_in, down_total)

    @pl.when(low_ref[0] != 0)
    def _():
        extra_total[...] += one(up2_ref, up2_in, up2_total)
        down2_total[...] = down2_in[...]

    @pl.when(low_ref[0] == 0)
    def _():
        extra_total[...] += one(down2_ref, down2_in, down2_total)
        up2_total[...] = up2_in[...]


def extra_pairs(is_low, extra, blocks, sums):
    total = jax.ShapeDtypeStruct((COLS, BLK), jnp.float32)
    outs = pl.pallas_call(
        extra_body,
        out_shape=[total] * 6,
        in_specs=[pl.BlockSpec(memory_space=pltpu.SMEM)] + [VMEM] * 11,
        out_specs=[VMEM] * 6,
        compiler_params=pltpu.CompilerParams(vmem_limit_bytes=12 * 1024 * 1024),
        cost_estimate=cost(4, 6),
    )(is_low.astype(jnp.int32).reshape(1), extra, *blocks, *sums)
    return outs[:5], outs[5]


def on_device(spectra, scores):
    n = lax.axis_size(AXES)
    quads = n // 4
    me = lax.axis_index(AXES)
    column = lax.axis_size("gy") // 4
    level = (me >> 2) % column
    low, high = level < 2, level >= column - 2
    def route(block, source_of):
        return lax.ppermute(block, AXES, sources(source_of, n, column))

    def send(block, source_of):
        return lax.ppermute(block, AXES, [(i, source) for source, i in sources(source_of, n, column)])

    def swap(block, bits):
        return lax.ppermute(block, AXES, [(i, i ^ bits) for i in range(n)])

    zero = packed(spectra, scores)
    far = route(zero, far_source)
    up = route(zero, lambda i, column, quads: near_source(i, 1, 1, column, quads))
    down = route(zero, lambda i, column, quads: near_source(i, -1, 1, column, quads))
    up2 = route(up, lambda i, column, quads: near_source(i, 1, 2, column, quads))
    down2 = route(down, lambda i, column, quads: near_source(i, -1, 2, column, quads))
    back = route(jnp.where(back_level(me, column), far, up2), back_source)
    up2 = jnp.where(high, far, up2)
    beside = swap(up2, 2)
    across = swap(up2, 3)
    sibling = swap(up2, 1)
    up2, down2 = lax.optimization_barrier((up2, down2))
    down2 = jnp.where(low, far, down2)
    back, _, _ = lax.optimization_barrier((back, up2, down2))
    up = jnp.where(level == column - 1, back, up)
    down = jnp.where(level == 0, back, down)

    blocks = [zero, up, down, up2, down2]
    sums = pairs(blocks, ((0, 0), (0, 1), (2, 1), (2, 3), (4, 3)), (0, 1, 2, 3, 4))
    sums, for_beside = extra_pairs((me & 2) == 0, beside, blocks, sums)
    sums, for_sibling = extra_pairs((me & 1) == 0, sibling, blocks, sums)
    total, one, nine, two, eight = sums
    two = two + swap(for_sibling, 1) + swap(for_beside, 2)
    sums, for_across = extra_pairs((me & 2) == 0, across, blocks, [total, one, nine, two, eight])
    total, one, nine, two, eight = sums
    two = two + swap(for_across, 3)

    none = jnp.zeros_like(one)
    upward = send(
        jnp.concatenate([one, jnp.where(level == 0, nine, none)]),
        lambda i, column, quads: near_source(i, 1, 1, column, quads),
    )
    downward = send(
        jnp.concatenate([nine, jnp.where(level == column - 1, one, none)]),
        lambda i, column, quads: near_source(i, -1, 1, column, quads),
    )
    total = total + upward[:COLS] + downward[:COLS]
    crossing = jnp.where(high, two + downward[COLS:], eight + upward[COLS:])
    total = total + send(crossing, far_source)
    total = total + send(two, lambda i, column, quads: inner_source(i, 2, column, quads))
    eight = jnp.where(me < n, eight, crossing)
    total = total + send(eight, lambda i, column, quads: inner_source(i, -2, column, quads))
    return total.T


def solution(mesh):
    return jax.shard_map(
        on_device,
        mesh=mesh,
        in_specs=(P(AXES, None), P(AXES, None)),
        out_specs=P(AXES, None),
        check_vma=False,
    )
```

```python
import functools

import jax
import jax.numpy as jnp
from jax import lax
from jax.experimental import pallas as pl
from jax.experimental.pallas import tpu as pltpu
from jax.sharding import PartitionSpec as P

WAVE = 1024
BLK = 224
COLS = 32
PACK = 16
AXES = ("gx", "gy")

spread_rate = 4.0


def split(i):
    return i >> 2, (i >> 1) & 1, i & 1


def device(quad, side, core, quads):
    return (quad % quads) * 4 + side * 2 + core


def stepped(i, j, quads):
    quad, side, core = split(i)
    return device(quad + j, side, core, quads)


def within(i, j, column, quads):
    return stepped(i, j, quads) // (4 * column) == i // (4 * column)


def near_source(i, j, steps, column, quads):
    return stepped(i, j, quads) if within(i, j * steps, column, quads) else None


def inner_source(i, j, column, quads):
    return stepped(i, j, quads) if within(i, j, column, quads) else None


def far_source(i, column, quads):
    for j in (2, -2):
        if not within(i, j, column, quads):
            return stepped(i, j, quads)
    return None


def back_level(me, column):
    level = (me >> 2) % column
    return (level == 1) | (level == column - 2)


def back_source(i, column, quads):
    for j in (1, -1):
        if not within(i, j, column, quads):
            return stepped(i, -j, quads)
    return None


def sources(source_of, n, column):
    found = [(source_of(i, column, n // 4), i) for i in range(n)]
    return [(source, i) for source, i in found if source is not None]


VMEM = pl.BlockSpec(memory_space=pltpu.VMEM)


def packed_body(spectra_ref, scores_ref, out_ref):
    out_ref[0:BLK, :] = spectra_ref[...]
    turned = scores_ref[...].astype(jnp.float32).T.astype(jnp.bfloat16)
    out_ref[BLK:BLK + PACK, :] = jnp.zeros((PACK, WAVE), jnp.bfloat16)
    out_ref[BLK:BLK + PACK, 0:BLK] = turned[0:PACK]
    out_ref[BLK:BLK + PACK, 256:256 + BLK] = turned[PACK:COLS]


def packed(spectra, scores):
    return pl.pallas_call(
        packed_body,
        out_shape=jax.ShapeDtypeStruct((BLK + PACK, WAVE), jnp.bfloat16),
        in_specs=[VMEM] * 2,
        out_specs=VMEM,
        compiler_params=pltpu.CompilerParams(vmem_limit_bytes=12 * 1024 * 1024),
        cost_estimate=pl.CostEstimate(flops=0, bytes_accessed=4 * BLK * WAVE, transcendentals=0),
    )(spectra, scores)


def rows_of(ref):
    return ref[0:BLK, :]


def scores_of(ref):
    return jnp.concatenate([ref[BLK:BLK + PACK, 0:BLK], ref[BLK:BLK + PACK, 256:256 + BLK]], axis=0)


def norms_of(ref):
    x = rows_of(ref).astype(jnp.float32)
    column = jnp.sum(x * x, axis=1, keepdims=True)
    row = jnp.broadcast_to(column, (BLK, 128)).T[0:1, :]
    return column, row


def tile_of(a_ref, a_column, b_ref, b_row):
    cross = lax.dot_general(
        rows_of(a_ref), rows_of(b_ref), (((1,), (1,)), ((), ())), preferred_element_type=jnp.float32
    )
    dist = a_column + b_row - 2.0 * cross
    return jnp.exp(-spread_rate * dist / WAVE).astype(jnp.bfloat16)


def to_rows(kern, b_scores):
    return lax.dot_general(b_scores, kern, (((1,), (1,)), ((), ())), preferred_element_type=jnp.float32)


def to_columns(kern, a_scores):
    return jnp.dot(a_scores, kern, preferred_element_type=jnp.float32)


def pairs_body(tiles, outs, known, *refs):
    count = len(refs) - len(outs) - len(known)
    blocks, before, totals = refs[:count], refs[count:count + len(known)], refs[count + len(known):]
    used = sorted({t for tile in tiles for t in tile})
    norms = {t: norms_of(blocks[t]) for t in used}
    scores = {t: scores_of(blocks[t]) for t in used}
    sums = {t: ref[...] for t, ref in zip(known, before)}

    def add(t, value):
        sums[t] = value if t not in sums else sums[t] + value

    for a, b in tiles:
        kern = tile_of(blocks[a], norms[a][0], blocks[b], norms[b][1])
        add(a, to_rows(kern, scores[b]))
        if a != b:
            add(b, to_columns(kern, scores[a]))
    for t, total in zip(outs, totals):
        total[...] = sums[t]


def cost(tiles, blocks):
    return pl.CostEstimate(
        flops=tiles * 2 * BLK * BLK * (WAVE + 2 * COLS),
        bytes_accessed=blocks * (BLK + PACK) * WAVE * 2,
        transcendentals=tiles * BLK * BLK,
    )


def pairs(blocks, tiles, outs, known, sums):
    return pl.pallas_call(
        functools.partial(pairs_body, tiles, outs, known),
        out_shape=[jax.ShapeDtypeStruct((COLS, BLK), jnp.float32)] * len(outs),
        in_specs=[VMEM] * (len(blocks) + len(sums)),
        out_specs=[VMEM] * len(outs),
        compiler_params=pltpu.CompilerParams(vmem_limit_bytes=12 * 1024 * 1024),
        cost_estimate=cost(len(tiles), len(blocks)),
    )(*blocks, *sums)


def extra_body(
    low_ref, extra_ref, zero_ref, up_ref, down_ref, up2_ref, down2_ref,
    zero_in, up_in, down_in, up2_in, down2_in,
    zero_total, up_total, down_total, up2_total, down2_total, extra_total,
):
    column, _ = norms_of(extra_ref)
    extra_scores = scores_of(extra_ref)

    def one(ref, before, after):
        kern = tile_of(extra_ref, column, ref, norms_of(ref)[1])
        after[...] = before[...] + to_columns(kern, extra_scores)
        return to_rows(kern, scores_of(ref))

    mine = one(zero_ref, zero_in, zero_total)
    mine = mine + one(up_ref, up_in, up_total)
    extra_total[...] = mine + one(down_ref, down_in, down_total)

    @pl.when(low_ref[0] != 0)
    def _():
        extra_total[...] += one(up2_ref, up2_in, up2_total)
        down2_total[...] = down2_in[...]

    @pl.when(low_ref[0] == 0)
    def _():
        extra_total[...] += one(down2_ref, down2_in, down2_total)
        up2_total[...] = up2_in[...]


def extra_pairs(is_low, extra, blocks, sums):
    total = jax.ShapeDtypeStruct((COLS, BLK), jnp.float32)
    outs = pl.pallas_call(
        extra_body,
        out_shape=[total] * 6,
        in_specs=[pl.BlockSpec(memory_space=pltpu.SMEM)] + [VMEM] * 11,
        out_specs=[VMEM] * 6,
        compiler_params=pltpu.CompilerParams(vmem_limit_bytes=12 * 1024 * 1024),
        cost_estimate=cost(4, 6),
    )(is_low.astype(jnp.int32).reshape(1), extra, *blocks, *sums)
    return outs[:5], outs[5]


def early_body(low_ref, extra_ref, zero_ref, up2_ref, down2_ref,
               zero_total, up2_total, down2_total, extra_total, chosen_ref):
    low = low_ref[0] != 0

    @pl.when(low)
    def _():
        chosen_ref[...] = up2_ref[...]

    @pl.when(jnp.logical_not(low))
    def _():
        chosen_ref[...] = down2_ref[...]

    zero_column, zero_row = norms_of(zero_ref)
    zero_scores = scores_of(zero_ref)
    total = to_rows(tile_of(zero_ref, zero_column, zero_ref, zero_row), zero_scores)
    kern = tile_of(down2_ref, norms_of(down2_ref)[0], up2_ref, norms_of(up2_ref)[1])
    down2_sum = to_rows(kern, scores_of(up2_ref))
    up2_sum = to_columns(kern, scores_of(down2_ref))
    column, _ = norms_of(extra_ref)
    scores = scores_of(extra_ref)
    kern = tile_of(extra_ref, column, zero_ref, zero_row)
    mine = to_rows(kern, zero_scores)
    zero_total[...] = total + to_columns(kern, scores)
    kern = tile_of(extra_ref, column, chosen_ref, norms_of(chosen_ref)[1])
    extra_total[...] = mine + to_rows(kern, scores_of(chosen_ref))
    theirs = to_columns(kern, scores)
    up2_total[...] = up2_sum + jnp.where(low, theirs, 0.0)
    down2_total[...] = down2_sum + jnp.where(low, 0.0, theirs)


def early_pairs(is_low, blocks):
    return pl.pallas_call(
        early_body,
        out_shape=[jax.ShapeDtypeStruct((COLS, BLK), jnp.float32)] * 4,
        in_specs=[pl.BlockSpec(memory_space=pltpu.SMEM)] + [VMEM] * 4,
        out_specs=[VMEM] * 4,
        scratch_shapes=[pltpu.VMEM((BLK + PACK, WAVE), jnp.bfloat16)],
        compiler_params=pltpu.CompilerParams(vmem_limit_bytes=12 * 1024 * 1024),
        cost_estimate=cost(4, 4),
    )(is_low.astype(jnp.int32).reshape(1), *blocks)


def on_device(spectra, scores):
    n = lax.axis_size(AXES)
    quads = n // 4
    me = lax.axis_index(AXES)
    column = lax.axis_size("gy") // 4
    level = (me >> 2) % column
    low, high = level < 2, level >= column - 2
    def route(block, source_of):
        return lax.ppermute(block, AXES, sources(source_of, n, column))

    def send(block, source_of):
        return lax.ppermute(block, AXES, [(i, source) for source, i in sources(source_of, n, column)])

    def swap(block, bits):
        return lax.ppermute(block, AXES, [(i, i ^ bits) for i in range(n)])

    zero = packed(spectra, scores)
    far = route(zero, far_source)
    up = route(zero, lambda i, column, quads: near_source(i, 1, 1, column, quads))
    down = route(zero, lambda i, column, quads: near_source(i, -1, 1, column, quads))
    up2 = route(up, lambda i, column, quads: near_source(i, 1, 2, column, quads))
    down2 = route(down, lambda i, column, quads: near_source(i, -1, 2, column, quads))
    back = route(jnp.where(back_level(me, column), far, up2), back_source)
    up2 = jnp.where(high, far, up2)
    beside = swap(up2, 2)
    sibling = swap(up2, 1)
    up2, down2 = lax.optimization_barrier((up2, down2))
    down2 = jnp.where(low, far, down2)
    back, _, _ = lax.optimization_barrier((back, up2, down2))
    total, two, eight, for_sibling = early_pairs((me & 1) == 0, [sibling, zero, up2, down2])
    across = swap(jnp.where((me < n) | (total[0, 0] > 0), beside, up2), 1)
    up = jnp.where(level == column - 1, back, up)
    down = jnp.where(level == 0, back, down)

    total, one, nine, two, for_sibling = pairs(
        [zero, up, down, up2, sibling],
        ((0, 1), (2, 1), (2, 3), (4, 1), (4, 2)),
        (0, 1, 2, 3, 4),
        (0, 3, 4),
        [total, two, for_sibling],
    )
    blocks = [zero, up, down, up2, down2]
    sums, for_beside = extra_pairs((me & 2) == 0, beside, blocks, [total, one, nine, two, eight])
    sums, for_across = extra_pairs((me & 2) == 0, across, blocks, sums)
    total, one, nine, two, eight = sums
    two = two + swap(for_sibling, 1) + swap(for_beside, 2) + swap(for_across, 3)

    none = jnp.zeros_like(one)
    upward = send(
        jnp.concatenate([one, jnp.where(level == 0, nine, none)]),
        lambda i, column, quads: near_source(i, 1, 1, column, quads),
    )
    downward = send(
        jnp.concatenate([nine, jnp.where(level == column - 1, one, none)]),
        lambda i, column, quads: near_source(i, -1, 1, column, quads),
    )
    total = total + upward[:COLS] + downward[:COLS]
    crossing = jnp.where(high, two + downward[COLS:], eight + upward[COLS:])
    total = total + send(crossing, far_source)
    total = total + send(two, lambda i, column, quads: inner_source(i, 2, column, quads))
    eight = jnp.where(me < n, eight, crossing)
    total = total + send(eight, lambda i, column, quads: inner_source(i, -2, column, quads))
    return total.T


def solution(mesh):
    return jax.shard_map(
        on_device,
        mesh=mesh,
        in_specs=(P(AXES, None), P(AXES, None)),
        out_specs=P(AXES, None),
        check_vma=False,
    )
```

```python
import functools

import jax
import jax.numpy as jnp
from jax import lax
from jax.experimental import pallas as pl
from jax.experimental.pallas import tpu as pltpu
from jax.sharding import PartitionSpec as P

WAVE = 1024
BLK = 224
COLS = 32
PACK = 16
AXES = ("gx", "gy")

spread_rate = 4.0


def split(i):
    return i >> 2, (i >> 1) & 1, i & 1


def device(quad, side, core, quads):
    return (quad % quads) * 4 + side * 2 + core


def stepped(i, j, quads):
    quad, side, core = split(i)
    return device(quad + j, side, core, quads)


def within(i, j, column, quads):
    return stepped(i, j, quads) // (4 * column) == i // (4 * column)


def near_source(i, j, steps, column, quads):
    return stepped(i, j, quads) if within(i, j * steps, column, quads) else None


def inner_source(i, j, column, quads):
    return stepped(i, j, quads) if within(i, j, column, quads) else None


def far_source(i, column, quads):
    for j in (2, -2):
        if not within(i, j, column, quads):
            return stepped(i, j, quads)
    return None


def back_level(me, column):
    level = (me >> 2) % column
    return (level == 1) | (level == column - 2)


def back_source(i, column, quads):
    for j in (1, -1):
        if not within(i, j, column, quads):
            return stepped(i, -j, quads)
    return None


def sources(source_of, n, column):
    found = [(source_of(i, column, n // 4), i) for i in range(n)]
    return [(source, i) for source, i in found if source is not None]


VMEM = pl.BlockSpec(memory_space=pltpu.VMEM)


def packed_body(spectra_ref, scores_ref, out_ref):
    out_ref[0:BLK, :] = spectra_ref[...]
    turned = scores_ref[...].astype(jnp.float32).T.astype(jnp.bfloat16)
    out_ref[BLK:BLK + PACK, :] = jnp.zeros((PACK, WAVE), jnp.bfloat16)
    out_ref[BLK:BLK + PACK, 0:BLK] = turned[0:PACK]
    out_ref[BLK:BLK + PACK, 256:256 + BLK] = turned[PACK:COLS]


def packed(spectra, scores):
    return pl.pallas_call(
        packed_body,
        out_shape=jax.ShapeDtypeStruct((BLK + PACK, WAVE), jnp.bfloat16),
        in_specs=[VMEM] * 2,
        out_specs=VMEM,
        compiler_params=pltpu.CompilerParams(vmem_limit_bytes=12 * 1024 * 1024),
        cost_estimate=pl.CostEstimate(flops=0, bytes_accessed=4 * BLK * WAVE, transcendentals=0),
    )(spectra, scores)


def rows_of(ref):
    return ref[0:BLK, :]


def scores_of(ref):
    return jnp.concatenate([ref[BLK:BLK + PACK, 0:BLK], ref[BLK:BLK + PACK, 256:256 + BLK]], axis=0)


def norms_of(ref):
    x = rows_of(ref).astype(jnp.float32)
    column = jnp.sum(x * x, axis=1, keepdims=True)
    row = jnp.broadcast_to(column, (BLK, 128)).T[0:1, :]
    return column, row


def tile_of(a_ref, a_column, b_ref, b_row):
    cross = lax.dot_general(
        rows_of(a_ref), rows_of(b_ref), (((1,), (1,)), ((), ())), preferred_element_type=jnp.float32
    )
    dist = a_column + b_row - 2.0 * cross
    return jnp.exp(-spread_rate * dist / WAVE).astype(jnp.bfloat16)


def to_rows(kern, b_scores):
    return lax.dot_general(b_scores, kern, (((1,), (1,)), ((), ())), preferred_element_type=jnp.float32)


def to_columns(kern, a_scores):
    return jnp.dot(a_scores, kern, preferred_element_type=jnp.float32)


def pairs_body(tiles, outs, known, *refs):
    count = len(refs) - len(outs) - len(known)
    blocks, before, totals = refs[:count], refs[count:count + len(known)], refs[count + len(known):]
    used = sorted({t for tile in tiles for t in tile})
    norms = {t: norms_of(blocks[t]) for t in used}
    scores = {t: scores_of(blocks[t]) for t in used}
    sums = {t: ref[...] for t, ref in zip(known, before)}

    def add(t, value):
        sums[t] = value if t not in sums else sums[t] + value

    for a, b in tiles:
        kern = tile_of(blocks[a], norms[a][0], blocks[b], norms[b][1])
        add(a, to_rows(kern, scores[b]))
        if a != b:
            add(b, to_columns(kern, scores[a]))
    for t, total in zip(outs, totals):
        total[...] = sums[t]


def cost(tiles, blocks):
    return pl.CostEstimate(
        flops=tiles * 2 * BLK * BLK * (WAVE + 2 * COLS),
        bytes_accessed=blocks * (BLK + PACK) * WAVE * 2,
        transcendentals=tiles * BLK * BLK,
    )


def pairs(blocks, tiles, outs, known, sums):
    return pl.pallas_call(
        functools.partial(pairs_body, tiles, outs, known),
        out_shape=[jax.ShapeDtypeStruct((COLS, BLK), jnp.float32)] * len(outs),
        in_specs=[VMEM] * (len(blocks) + len(sums)),
        out_specs=[VMEM] * len(outs),
        compiler_params=pltpu.CompilerParams(vmem_limit_bytes=12 * 1024 * 1024),
        cost_estimate=cost(len(tiles), len(blocks)),
    )(*blocks, *sums)


def extra_body(
    low_ref, extra_ref, zero_ref, up_ref, down_ref, up2_ref, down2_ref,
    zero_in, up_in, down_in, up2_in, down2_in,
    zero_total, up_total, down_total, up2_total, down2_total, extra_total,
):
    column, _ = norms_of(extra_ref)
    extra_scores = scores_of(extra_ref)

    def one(ref, before, after):
        kern = tile_of(extra_ref, column, ref, norms_of(ref)[1])
        after[...] = before[...] + to_columns(kern, extra_scores)
        return to_rows(kern, scores_of(ref))

    mine = one(zero_ref, zero_in, zero_total)
    mine = mine + one(up_ref, up_in, up_total)
    extra_total[...] = mine + one(down_ref, down_in, down_total)

    @pl.when(low_ref[0] != 0)
    def _():
        extra_total[...] += one(up2_ref, up2_in, up2_total)
        down2_total[...] = down2_in[...]

    @pl.when(low_ref[0] == 0)
    def _():
        extra_total[...] += one(down2_ref, down2_in, down2_total)
        up2_total[...] = up2_in[...]


def extra_pairs(is_low, extra, blocks, sums):
    total = jax.ShapeDtypeStruct((COLS, BLK), jnp.float32)
    outs = pl.pallas_call(
        extra_body,
        out_shape=[total] * 6,
        in_specs=[pl.BlockSpec(memory_space=pltpu.SMEM)] + [VMEM] * 11,
        out_specs=[VMEM] * 6,
        compiler_params=pltpu.CompilerParams(vmem_limit_bytes=12 * 1024 * 1024),
        cost_estimate=cost(4, 6),
    )(is_low.astype(jnp.int32).reshape(1), extra, *blocks, *sums)
    return outs[:5], outs[5]


def early_body(low_ref, extra_ref, zero_ref, up2_ref, down2_ref,
               zero_total, up2_total, down2_total, extra_total, chosen_ref):
    low = low_ref[0] != 0

    @pl.when(low)
    def _():
        chosen_ref[...] = up2_ref[...]

    @pl.when(jnp.logical_not(low))
    def _():
        chosen_ref[...] = down2_ref[...]

    zero_column, zero_row = norms_of(zero_ref)
    zero_scores = scores_of(zero_ref)
    total = to_rows(tile_of(zero_ref, zero_column, zero_ref, zero_row), zero_scores)
    kern = tile_of(down2_ref, norms_of(down2_ref)[0], up2_ref, norms_of(up2_ref)[1])
    down2_sum = to_rows(kern, scores_of(up2_ref))
    up2_sum = to_columns(kern, scores_of(down2_ref))
    column, _ = norms_of(extra_ref)
    scores = scores_of(extra_ref)
    kern = tile_of(extra_ref, column, zero_ref, zero_row)
    mine = to_rows(kern, zero_scores)
    zero_total[...] = total + to_columns(kern, scores)
    kern = tile_of(extra_ref, column, chosen_ref, norms_of(chosen_ref)[1])
    extra_total[...] = mine + to_rows(kern, scores_of(chosen_ref))
    theirs = to_columns(kern, scores)
    up2_total[...] = up2_sum + jnp.where(low, theirs, 0.0)
    down2_total[...] = down2_sum + jnp.where(low, 0.0, theirs)


def early_pairs(is_low, blocks):
    return pl.pallas_call(
        early_body,
        out_shape=[jax.ShapeDtypeStruct((COLS, BLK), jnp.float32)] * 4,
        in_specs=[pl.BlockSpec(memory_space=pltpu.SMEM)] + [VMEM] * 4,
        out_specs=[VMEM] * 4,
        scratch_shapes=[pltpu.VMEM((BLK + PACK, WAVE), jnp.bfloat16)],
        compiler_params=pltpu.CompilerParams(vmem_limit_bytes=12 * 1024 * 1024),
        cost_estimate=cost(4, 4),
    )(is_low.astype(jnp.int32).reshape(1), *blocks)


def on_device(spectra, scores):
    n = lax.axis_size(AXES)
    quads = n // 4
    me = lax.axis_index(AXES)
    column = lax.axis_size("gy") // 4
    level = (me >> 2) % column
    low, high = level < 2, level >= column - 2
    def route(block, source_of):
        return lax.ppermute(block, AXES, sources(source_of, n, column))

    def send(block, source_of):
        return lax.ppermute(block, AXES, [(i, source) for source, i in sources(source_of, n, column)])

    def swap(block, bits):
        return lax.ppermute(block, AXES, [(i, i ^ bits) for i in range(n)])

    zero = packed(spectra, scores)
    far = route(zero, far_source)
    up = route(zero, lambda i, column, quads: near_source(i, 1, 1, column, quads))
    down = route(zero, lambda i, column, quads: near_source(i, -1, 1, column, quads))
    up2 = route(up, lambda i, column, quads: near_source(i, 1, 2, column, quads))
    down2 = route(down, lambda i, column, quads: near_source(i, -1, 2, column, quads))
    back = route(jnp.where(back_level(me, column), far, up2), back_source)
    up2 = jnp.where(high, far, up2)
    beside = swap(up2, 2)
    sibling = swap(up2, 1)
    across = swap(beside, 1)
    up2, down2 = lax.optimization_barrier((up2, down2))
    down2 = jnp.where(low, far, down2)
    back, _, _ = lax.optimization_barrier((back, up2, down2))
    up = jnp.where(level == column - 1, back, up)
    down = jnp.where(level == 0, back, down)

    total, two, eight, for_sibling = early_pairs((me & 1) == 0, [sibling, zero, up2, down2])
    total, one, nine, two, for_sibling = pairs(
        [zero, up, down, up2, sibling],
        ((0, 1), (2, 1), (2, 3), (4, 1), (4, 2)),
        (0, 1, 2, 3, 4),
        (0, 3, 4),
        [total, two, for_sibling],
    )
    blocks = [zero, up, down, up2, down2]
    sums, for_beside = extra_pairs((me & 2) == 0, beside, blocks, [total, one, nine, two, eight])
    sums, for_across = extra_pairs((me & 2) == 0, across, blocks, sums)
    total, one, nine, two, eight = sums
    handed = swap(jnp.concatenate([for_sibling, for_across]), 1)
    two = two + handed[:COLS] + swap(for_beside + handed[COLS:], 2)

    none = jnp.zeros_like(one)
    upward = send(
        jnp.concatenate([one, jnp.where(level == 0, nine, none)]),
        lambda i, column, quads: near_source(i, 1, 1, column, quads),
    )
    downward = send(
        jnp.concatenate([nine, jnp.where(level == column - 1, one, none)]),
        lambda i, column, quads: near_source(i, -1, 1, column, quads),
    )
    total = total + upward[:COLS] + downward[:COLS]
    crossing = jnp.where(high, two + downward[COLS:], eight + upward[COLS:])
    total = total + send(crossing, far_source)
    total = total + send(two, lambda i, column, quads: inner_source(i, 2, column, quads))
    eight = jnp.where(me < n, eight, crossing)
    total = total + send(eight, lambda i, column, quads: inner_source(i, -2, column, quads))
    return total.T


def solution(mesh):
    return jax.shard_map(
        on_device,
        mesh=mesh,
        in_specs=(P(AXES, None), P(AXES, None)),
        out_specs=P(AXES, None),
        check_vma=False,
    )
```

```python
import functools

import jax
import jax.numpy as jnp
from jax import lax
from jax.experimental import pallas as pl
from jax.experimental.pallas import tpu as pltpu
from jax.sharding import PartitionSpec as P

WAVE = 1024
BLK = 224
COLS = 32
PACK = 16
AXES = ("gx", "gy")

spread_rate = 4.0


def split(i):
    return i >> 2, (i >> 1) & 1, i & 1


def device(quad, side, core, quads):
    return (quad % quads) * 4 + side * 2 + core


def stepped(i, j, quads):
    quad, side, core = split(i)
    return device(quad + j, side, core, quads)


def within(i, j, column, quads):
    return stepped(i, j, quads) // (4 * column) == i // (4 * column)


def near_source(i, j, steps, column, quads):
    return stepped(i, j, quads) if within(i, j * steps, column, quads) else None


def inner_source(i, j, column, quads):
    return stepped(i, j, quads) if within(i, j, column, quads) else None


def far_source(i, column, quads):
    for j in (2, -2):
        if not within(i, j, column, quads):
            return stepped(i, j, quads)
    return None


def back_level(me, column):
    level = (me >> 2) % column
    return (level == 1) | (level == column - 2)


def back_source(i, column, quads):
    for j in (1, -1):
        if not within(i, j, column, quads):
            return stepped(i, -j, quads)
    return None


def sources(source_of, n, column):
    found = [(source_of(i, column, n // 4), i) for i in range(n)]
    return [(source, i) for source, i in found if source is not None]


VMEM = pl.BlockSpec(memory_space=pltpu.VMEM)
ROW = jax.ShapeDtypeStruct((1, BLK), jnp.float32)


def packed_body(spectra_ref, scores_ref, out_ref):
    out_ref[0:BLK, :] = spectra_ref[...]
    turned = scores_ref[...].astype(jnp.float32).T.astype(jnp.bfloat16)
    out_ref[BLK:BLK + PACK, :] = jnp.zeros((PACK, WAVE), jnp.bfloat16)
    out_ref[BLK:BLK + PACK, 0:BLK] = turned[0:PACK]
    out_ref[BLK:BLK + PACK, 256:256 + BLK] = turned[PACK:COLS]


def packed(spectra, scores):
    return pl.pallas_call(
        packed_body,
        out_shape=jax.ShapeDtypeStruct((BLK + PACK, WAVE), jnp.bfloat16),
        in_specs=[VMEM] * 2,
        out_specs=VMEM,
        compiler_params=pltpu.CompilerParams(vmem_limit_bytes=12 * 1024 * 1024),
        cost_estimate=pl.CostEstimate(flops=0, bytes_accessed=4 * BLK * WAVE, transcendentals=0),
    )(spectra, scores)


def rows_of(ref):
    return ref[0:BLK, :]


def scores_of(ref):
    return jnp.concatenate([ref[BLK:BLK + PACK, 0:BLK], ref[BLK:BLK + PACK, 256:256 + BLK]], axis=0)


def norms_of(ref):
    x = rows_of(ref).astype(jnp.float32)
    column = jnp.sum(x * x, axis=1, keepdims=True)
    row = jnp.broadcast_to(column, (BLK, 128)).T[0:1, :]
    return column, row


def tile_of(a_ref, a_column, b_ref, b_row):
    cross = lax.dot_general(
        rows_of(a_ref), rows_of(b_ref), (((1,), (1,)), ((), ())), preferred_element_type=jnp.float32
    )
    dist = a_column + b_row - 2.0 * cross
    return jnp.exp(-spread_rate * dist / WAVE).astype(jnp.bfloat16)


def to_rows(kern, b_scores):
    return lax.dot_general(b_scores, kern, (((1,), (1,)), ((), ())), preferred_element_type=jnp.float32)


def to_columns(kern, a_scores):
    return jnp.dot(a_scores, kern, preferred_element_type=jnp.float32)


def pairs_body(tiles, outs, known, rows, *refs):
    count = len(refs) - len(outs) - len(known) - len(rows)
    blocks, before, totals = refs[:count], refs[count:count + len(known)], refs[count + len(known):]
    used = sorted({t for tile in tiles for t in tile})
    norms = {t: norms_of(blocks[t]) for t in used}
    scores = {t: scores_of(blocks[t]) for t in used}
    sums = {t: ref[...] for t, ref in zip(known, before)}

    def add(t, value):
        sums[t] = value if t not in sums else sums[t] + value

    for a, b in tiles:
        kern = tile_of(blocks[a], norms[a][0], blocks[b], norms[b][1])
        add(a, to_rows(kern, scores[b]))
        if a != b:
            add(b, to_columns(kern, scores[a]))
    for t, total in zip(outs, totals):
        total[...] = sums[t]
    for t, row in zip(rows, totals[len(outs):]):
        row[...] = norms[t][1]


def cost(tiles, blocks):
    return pl.CostEstimate(
        flops=tiles * 2 * BLK * BLK * (WAVE + 2 * COLS),
        bytes_accessed=blocks * (BLK + PACK) * WAVE * 2,
        transcendentals=tiles * BLK * BLK,
    )


def pairs(blocks, tiles, outs, known, rows, sums):
    return pl.pallas_call(
        functools.partial(pairs_body, tiles, outs, known, rows),
        out_shape=[jax.ShapeDtypeStruct((COLS, BLK), jnp.float32)] * len(outs) + [ROW] * len(rows),
        in_specs=[VMEM] * (len(blocks) + len(sums)),
        out_specs=[VMEM] * (len(outs) + len(rows)),
        compiler_params=pltpu.CompilerParams(vmem_limit_bytes=12 * 1024 * 1024),
        cost_estimate=cost(len(tiles), len(blocks)),
    )(*blocks, *sums)


def extra_body(
    low_ref, extra_ref, zero_ref, up_ref, down_ref, up2_ref, down2_ref,
    zero_norms, up_norms, down_norms, up2_norms, down2_norms,
    zero_in, up_in, down_in, up2_in, down2_in,
    zero_total, up_total, down_total, up2_total, down2_total, extra_total,
):
    column, _ = norms_of(extra_ref)
    extra_scores = scores_of(extra_ref)

    def one(ref, norms, before, after):
        kern = tile_of(extra_ref, column, ref, norms[...])
        after[...] = before[...] + to_columns(kern, extra_scores)
        return to_rows(kern, scores_of(ref))

    mine = one(zero_ref, zero_norms, zero_in, zero_total)
    mine = mine + one(up_ref, up_norms, up_in, up_total)
    extra_total[...] = mine + one(down_ref, down_norms, down_in, down_total)

    @pl.when(low_ref[0] != 0)
    def _():
        extra_total[...] += one(up2_ref, up2_norms, up2_in, up2_total)
        down2_total[...] = down2_in[...]

    @pl.when(low_ref[0] == 0)
    def _():
        extra_total[...] += one(down2_ref, down2_norms, down2_in, down2_total)
        up2_total[...] = up2_in[...]


def extra_pairs(is_low, extra, blocks, norms, sums):
    total = jax.ShapeDtypeStruct((COLS, BLK), jnp.float32)
    outs = pl.pallas_call(
        extra_body,
        out_shape=[total] * 6,
        in_specs=[pl.BlockSpec(memory_space=pltpu.SMEM)] + [VMEM] * 16,
        out_specs=[VMEM] * 6,
        compiler_params=pltpu.CompilerParams(vmem_limit_bytes=12 * 1024 * 1024),
        cost_estimate=cost(4, 6),
    )(is_low.astype(jnp.int32).reshape(1), extra, *blocks, *norms, *sums)
    return outs[:5], outs[5]


def early_body(low_ref, extra_ref, zero_ref, up2_ref, down2_ref,
               zero_total, up2_total, down2_total, extra_total, zero_norms, up2_norms, down2_norms, chosen_ref):
    low = low_ref[0] != 0

    @pl.when(low)
    def _():
        chosen_ref[...] = up2_ref[...]

    @pl.when(jnp.logical_not(low))
    def _():
        chosen_ref[...] = down2_ref[...]

    zero_column, zero_row = norms_of(zero_ref)
    zero_scores = scores_of(zero_ref)
    total = to_rows(tile_of(zero_ref, zero_column, zero_ref, zero_row), zero_scores)
    _, up2_row = norms_of(up2_ref)
    down2_column, down2_row = norms_of(down2_ref)
    zero_norms[...], up2_norms[...], down2_norms[...] = zero_row, up2_row, down2_row
    kern = tile_of(down2_ref, down2_column, up2_ref, up2_row)
    down2_sum = to_rows(kern, scores_of(up2_ref))
    up2_sum = to_columns(kern, scores_of(down2_ref))
    column, _ = norms_of(extra_ref)
    scores = scores_of(extra_ref)
    kern = tile_of(extra_ref, column, zero_ref, zero_row)
    mine = to_rows(kern, zero_scores)
    zero_total[...] = total + to_columns(kern, scores)
    kern = tile_of(extra_ref, column, chosen_ref, jnp.where(low, up2_row, down2_row))
    extra_total[...] = mine + to_rows(kern, scores_of(chosen_ref))
    theirs = to_columns(kern, scores)
    up2_total[...] = up2_sum + jnp.where(low, theirs, 0.0)
    down2_total[...] = down2_sum + jnp.where(low, 0.0, theirs)


def early_pairs(is_low, blocks):
    return pl.pallas_call(
        early_body,
        out_shape=[jax.ShapeDtypeStruct((COLS, BLK), jnp.float32)] * 4 + [ROW] * 3,
        in_specs=[pl.BlockSpec(memory_space=pltpu.SMEM)] + [VMEM] * 4,
        out_specs=[VMEM] * 7,
        scratch_shapes=[pltpu.VMEM((BLK + PACK, WAVE), jnp.bfloat16)],
        compiler_params=pltpu.CompilerParams(vmem_limit_bytes=12 * 1024 * 1024),
        cost_estimate=cost(4, 4),
    )(is_low.astype(jnp.int32).reshape(1), *blocks)


def on_device(spectra, scores):
    n = lax.axis_size(AXES)
    quads = n // 4
    me = lax.axis_index(AXES)
    column = lax.axis_size("gy") // 4
    level = (me >> 2) % column
    low, high = level < 2, level >= column - 2
    def route(block, source_of):
        return lax.ppermute(block, AXES, sources(source_of, n, column))

    def send(block, source_of):
        return lax.ppermute(block, AXES, [(i, source) for source, i in sources(source_of, n, column)])

    def swap(block, bits):
        return lax.ppermute(block, AXES, [(i, i ^ bits) for i in range(n)])

    zero = packed(spectra, scores)
    far = route(zero, far_source)
    up = route(zero, lambda i, column, quads: near_source(i, 1, 1, column, quads))
    down = route(zero, lambda i, column, quads: near_source(i, -1, 1, column, quads))
    up2 = route(up, lambda i, column, quads: near_source(i, 1, 2, column, quads))
    down2 = route(down, lambda i, column, quads: near_source(i, -1, 2, column, quads))
    back = route(jnp.where(back_level(me, column), far, up2), back_source)
    up2 = jnp.where(high, far, up2)
    beside = swap(up2, 2)
    sibling = swap(up2, 1)
    across = swap(beside, 1)
    up2, down2 = lax.optimization_barrier((up2, down2))
    down2 = jnp.where(low, far, down2)
    back, _, _ = lax.optimization_barrier((back, up2, down2))
    up = jnp.where(level == column - 1, back, up)
    down = jnp.where(level == 0, back, down)

    total, two, eight, for_sibling, zero_norms, up2_norms, down2_norms = early_pairs(
        (me & 1) == 0, [sibling, zero, up2, down2]
    )
    total, one, nine, two, for_sibling, up_norms, down_norms = pairs(
        [zero, up, down, up2, sibling],
        ((0, 1), (2, 1), (2, 3), (4, 1), (4, 2)),
        (0, 1, 2, 3, 4),
        (0, 3, 4),
        (1, 2),
        [total, two, for_sibling],
    )
    blocks = [zero, up, down, up2, down2]
    norms = [zero_norms, up_norms, down_norms, up2_norms, down2_norms]
    sums, for_beside = extra_pairs((me & 2) == 0, beside, blocks, norms, [total, one, nine, two, eight])
    sums, for_across = extra_pairs((me & 2) == 0, across, blocks, norms, sums)
    total, one, nine, two, eight = sums
    handed = swap(jnp.concatenate([for_sibling, for_across]), 1)
    two = two + handed[:COLS] + swap(for_beside + handed[COLS:], 2)

    none = jnp.zeros_like(one)
    upward = send(
        jnp.concatenate([one, jnp.where(level == 0, nine, none)]),
        lambda i, column, quads: near_source(i, 1, 1, column, quads),
    )
    downward = send(
        jnp.concatenate([nine, jnp.where(level == column - 1, one, none)]),
        lambda i, column, quads: near_source(i, -1, 1, column, quads),
    )
    total = total + upward[:COLS] + downward[:COLS]
    crossing = jnp.where(high, two + downward[COLS:], eight + upward[COLS:])
    far_sums = send(eight, lambda i, column, quads: inner_source(i, -2, column, quads))
    far_sums = far_sums + send(two, lambda i, column, quads: inner_source(i, 2, column, quads))
    total = total + far_sums + send(crossing, far_source)
    return total.T


def solution(mesh):
    return jax.shard_map(
        on_device,
        mesh=mesh,
        in_specs=(P(AXES, None), P(AXES, None)),
        out_specs=P(AXES, None),
        check_vma=False,
    )
```

```python
import functools

import jax
import jax.numpy as jnp
from jax import lax
from jax.experimental import pallas as pl
from jax.experimental.pallas import tpu as pltpu
from jax.sharding import PartitionSpec as P

WAVE = 1024
BLK = 224
COLS = 32
PACK = 16
AXES = ("gx", "gy")

spread_rate = 4.0


def split(i):
    return i >> 2, (i >> 1) & 1, i & 1


def device(quad, side, core, quads):
    return (quad % quads) * 4 + side * 2 + core


def stepped(i, j, quads):
    quad, side, core = split(i)
    return device(quad + j, side, core, quads)


def within(i, j, column, quads):
    return stepped(i, j, quads) // (4 * column) == i // (4 * column)


def near_source(i, j, steps, column, quads):
    return stepped(i, j, quads) if within(i, j * steps, column, quads) else None


def inner_source(i, j, column, quads):
    return stepped(i, j, quads) if within(i, j, column, quads) else None


def far_source(i, column, quads):
    for j in (2, -2):
        if not within(i, j, column, quads):
            return stepped(i, j, quads)
    return None


def back_level(me, column):
    level = (me >> 2) % column
    return (level == 1) | (level == column - 2)


def back_source(i, column, quads):
    for j in (1, -1):
        if not within(i, j, column, quads):
            return stepped(i, -j, quads)
    return None


def sources(source_of, n, column):
    found = [(source_of(i, column, n // 4), i) for i in range(n)]
    return [(source, i) for source, i in found if source is not None]


VMEM = pl.BlockSpec(memory_space=pltpu.VMEM)
ROW = jax.ShapeDtypeStruct((1, BLK), jnp.float32)


def packed_body(spectra_ref, scores_ref, out_ref):
    out_ref[0:BLK, :] = spectra_ref[...]
    turned = scores_ref[...].astype(jnp.float32).T.astype(jnp.bfloat16)
    out_ref[BLK:BLK + PACK, :] = jnp.zeros((PACK, WAVE), jnp.bfloat16)
    out_ref[BLK:BLK + PACK, 0:BLK] = turned[0:PACK]
    out_ref[BLK:BLK + PACK, 256:256 + BLK] = turned[PACK:COLS]


def packed(spectra, scores):
    return pl.pallas_call(
        packed_body,
        out_shape=jax.ShapeDtypeStruct((BLK + PACK, WAVE), jnp.bfloat16),
        in_specs=[VMEM] * 2,
        out_specs=VMEM,
        compiler_params=pltpu.CompilerParams(vmem_limit_bytes=12 * 1024 * 1024),
        cost_estimate=pl.CostEstimate(flops=0, bytes_accessed=4 * BLK * WAVE, transcendentals=0),
    )(spectra, scores)


def pick_body(which_ref, one_ref, other_ref, out_ref):
    @pl.when(which_ref[0] != 0)
    def _():
        out_ref[...] = one_ref[...]

    @pl.when(which_ref[0] == 0)
    def _():
        out_ref[...] = other_ref[...]


def pick(which, one, other):
    return pl.pallas_call(
        pick_body,
        out_shape=jax.ShapeDtypeStruct(one.shape, one.dtype),
        in_specs=[pl.BlockSpec(memory_space=pltpu.SMEM)] + [VMEM] * 2,
        out_specs=VMEM,
        compiler_params=pltpu.CompilerParams(vmem_limit_bytes=12 * 1024 * 1024),
        cost_estimate=pl.CostEstimate(flops=0, bytes_accessed=4 * BLK * WAVE, transcendentals=0),
    )(which.astype(jnp.int32).reshape(1), one, other)


def rows_of(ref):
    return ref[0:BLK, :]


def scores_of(ref):
    return jnp.concatenate([ref[BLK:BLK + PACK, 0:BLK], ref[BLK:BLK + PACK, 256:256 + BLK]], axis=0)


def norms_of(ref):
    x = rows_of(ref).astype(jnp.float32)
    column = jnp.sum(x * x, axis=1, keepdims=True)
    row = jnp.broadcast_to(column, (BLK, 128)).T[0:1, :]
    return column, row


def tile_of(a_ref, a_column, b_ref, b_row):
    cross = lax.dot_general(
        rows_of(a_ref), rows_of(b_ref), (((1,), (1,)), ((), ())), preferred_element_type=jnp.float32
    )
    dist = a_column + b_row - 2.0 * cross
    return jnp.exp(-spread_rate * dist / WAVE).astype(jnp.bfloat16)


def to_rows(kern, b_scores):
    return lax.dot_general(b_scores, kern, (((1,), (1,)), ((), ())), preferred_element_type=jnp.float32)


def to_columns(kern, a_scores):
    return jnp.dot(a_scores, kern, preferred_element_type=jnp.float32)


def pairs_body(tiles, outs, known, rows, *refs):
    count = len(refs) - len(outs) - len(known) - len(rows)
    blocks, before, totals = refs[:count], refs[count:count + len(known)], refs[count + len(known):]
    used = sorted({t for tile in tiles for t in tile})
    norms = {t: norms_of(blocks[t]) for t in used}
    scores = {t: scores_of(blocks[t]) for t in used}
    sums = {t: ref[...] for t, ref in zip(known, before)}

    def add(t, value):
        sums[t] = value if t not in sums else sums[t] + value

    for a, b in tiles:
        kern = tile_of(blocks[a], norms[a][0], blocks[b], norms[b][1])
        add(a, to_rows(kern, scores[b]))
        if a != b:
            add(b, to_columns(kern, scores[a]))
    for t, total in zip(outs, totals):
        total[...] = sums[t]
    for t, row in zip(rows, totals[len(outs):]):
        row[...] = norms[t][1]


def cost(tiles, blocks):
    return pl.CostEstimate(
        flops=tiles * 2 * BLK * BLK * (WAVE + 2 * COLS),
        bytes_accessed=blocks * (BLK + PACK) * WAVE * 2,
        transcendentals=tiles * BLK * BLK,
    )


def pairs(blocks, tiles, outs, known, rows, sums):
    return pl.pallas_call(
        functools.partial(pairs_body, tiles, outs, known, rows),
        out_shape=[jax.ShapeDtypeStruct((COLS, BLK), jnp.float32)] * len(outs) + [ROW] * len(rows),
        in_specs=[VMEM] * (len(blocks) + len(sums)),
        out_specs=[VMEM] * (len(outs) + len(rows)),
        compiler_params=pltpu.CompilerParams(vmem_limit_bytes=12 * 1024 * 1024),
        cost_estimate=cost(len(tiles), len(blocks)),
    )(*blocks, *sums)


def extra_body(
    low_ref, extra_ref, zero_ref, up_ref, down_ref, up2_ref, down2_ref,
    zero_norms, up_norms, down_norms, up2_norms, down2_norms,
    zero_in, up_in, down_in, up2_in, down2_in,
    zero_total, up_total, down_total, up2_total, down2_total, extra_total,
):
    column, _ = norms_of(extra_ref)
    extra_scores = scores_of(extra_ref)

    def one(ref, norms, before, after):
        kern = tile_of(extra_ref, column, ref, norms[...])
        after[...] = before[...] + to_columns(kern, extra_scores)
        return to_rows(kern, scores_of(ref))

    mine = one(zero_ref, zero_norms, zero_in, zero_total)
    mine = mine + one(up_ref, up_norms, up_in, up_total)
    extra_total[...] = mine + one(down_ref, down_norms, down_in, down_total)

    @pl.when(low_ref[0] != 0)
    def _():
        extra_total[...] += one(up2_ref, up2_norms, up2_in, up2_total)
        down2_total[...] = down2_in[...]

    @pl.when(low_ref[0] == 0)
    def _():
        extra_total[...] += one(down2_ref, down2_norms, down2_in, down2_total)
        up2_total[...] = up2_in[...]


def extra_pairs(is_low, extra, blocks, norms, sums):
    total = jax.ShapeDtypeStruct((COLS, BLK), jnp.float32)
    outs = pl.pallas_call(
        extra_body,
        out_shape=[total] * 6,
        in_specs=[pl.BlockSpec(memory_space=pltpu.SMEM)] + [VMEM] * 16,
        out_specs=[VMEM] * 6,
        compiler_params=pltpu.CompilerParams(vmem_limit_bytes=12 * 1024 * 1024),
        cost_estimate=cost(4, 6),
    )(is_low.astype(jnp.int32).reshape(1), extra, *blocks, *norms, *sums)
    return outs[:5], outs[5]


def early_body(low_ref, extra_ref, zero_ref, up2_ref, down2_ref,
               zero_total, up2_total, down2_total, extra_total, zero_norms, up2_norms, down2_norms, chosen_ref):
    low = low_ref[0] != 0

    @pl.when(low)
    def _():
        chosen_ref[...] = up2_ref[...]

    @pl.when(jnp.logical_not(low))
    def _():
        chosen_ref[...] = down2_ref[...]

    zero_column, zero_row = norms_of(zero_ref)
    zero_scores = scores_of(zero_ref)
    total = to_rows(tile_of(zero_ref, zero_column, zero_ref, zero_row), zero_scores)
    _, up2_row = norms_of(up2_ref)
    down2_column, down2_row = norms_of(down2_ref)
    zero_norms[...], up2_norms[...], down2_norms[...] = zero_row, up2_row, down2_row
    kern = tile_of(down2_ref, down2_column, up2_ref, up2_row)
    down2_sum = to_rows(kern, scores_of(up2_ref))
    up2_sum = to_columns(kern, scores_of(down2_ref))
    column, _ = norms_of(extra_ref)
    scores = scores_of(extra_ref)
    kern = tile_of(extra_ref, column, zero_ref, zero_row)
    mine = to_rows(kern, zero_scores)
    zero_total[...] = total + to_columns(kern, scores)
    kern = tile_of(extra_ref, column, chosen_ref, jnp.where(low, up2_row, down2_row))
    extra_total[...] = mine + to_rows(kern, scores_of(chosen_ref))
    theirs = to_columns(kern, scores)
    up2_total[...] = up2_sum + jnp.where(low, theirs, 0.0)
    down2_total[...] = down2_sum + jnp.where(low, 0.0, theirs)


def early_pairs(is_low, blocks):
    return pl.pallas_call(
        early_body,
        out_shape=[jax.ShapeDtypeStruct((COLS, BLK), jnp.float32)] * 4 + [ROW] * 3,
        in_specs=[pl.BlockSpec(memory_space=pltpu.SMEM)] + [VMEM] * 4,
        out_specs=[VMEM] * 7,
        scratch_shapes=[pltpu.VMEM((BLK + PACK, WAVE), jnp.bfloat16)],
        compiler_params=pltpu.CompilerParams(vmem_limit_bytes=12 * 1024 * 1024),
        cost_estimate=cost(4, 4),
    )(is_low.astype(jnp.int32).reshape(1), *blocks)


def on_device(spectra, scores):
    n = lax.axis_size(AXES)
    quads = n // 4
    me = lax.axis_index(AXES)
    column = lax.axis_size("gy") // 4
    level = (me >> 2) % column
    low, high = level < 2, level >= column - 2
    def route(block, source_of):
        return lax.ppermute(block, AXES, sources(source_of, n, column))

    def send(block, source_of):
        return lax.ppermute(block, AXES, [(i, source) for source, i in sources(source_of, n, column)])

    def swap(block, bits):
        return lax.ppermute(block, AXES, [(i, i ^ bits) for i in range(n)])

    zero = packed(spectra, scores)
    far = route(zero, far_source)
    up = route(zero, lambda i, column, quads: near_source(i, 1, 1, column, quads))
    down = route(zero, lambda i, column, quads: near_source(i, -1, 1, column, quads))
    up2 = route(up, lambda i, column, quads: near_source(i, 1, 2, column, quads))
    down2 = route(down, lambda i, column, quads: near_source(i, -1, 2, column, quads))
    back = route(jnp.where(back_level(me, column), far, up2), back_source)
    up2 = pick(high, far, up2)
    beside = swap(up2, 2)
    sibling = swap(up2, 1)
    across = swap(beside, 1)
    up2, down2 = lax.optimization_barrier((up2, down2))
    down2 = jnp.where(low, far, down2)
    back, _, _ = lax.optimization_barrier((back, up2, down2))
    up = pick(level == column - 1, back, up)
    down = pick(level == 0, back, down)

    total, two, eight, for_sibling, zero_norms, up2_norms, down2_norms = early_pairs(
        (me & 1) == 0, [sibling, zero, up2, down2]
    )
    total, one, nine, two, for_sibling, up_norms, down_norms = pairs(
        [zero, up, down, up2, sibling],
        ((0, 1), (2, 1), (2, 3), (4, 1), (4, 2)),
        (0, 1, 2, 3, 4),
        (0, 3, 4),
        (1, 2),
        [total, two, for_sibling],
    )
    blocks = [zero, up, down, up2, down2]
    norms = [zero_norms, up_norms, down_norms, up2_norms, down2_norms]
    sums, for_beside = extra_pairs((me & 2) == 0, beside, blocks, norms, [total, one, nine, two, eight])
    sums, for_across = extra_pairs((me & 2) == 0, across, blocks, norms, sums)
    total, one, nine, two, eight = sums
    handed = swap(jnp.concatenate([for_sibling, for_across]), 1)
    two = two + handed[:COLS] + swap(for_beside + handed[COLS:], 2)

    none = jnp.zeros_like(one)
    upward = send(
        jnp.concatenate([one, jnp.where(level == 0, nine, none)]),
        lambda i, column, quads: near_source(i, 1, 1, column, quads),
    )
    downward = send(
        jnp.concatenate([nine, jnp.where(level == column - 1, one, none)]),
        lambda i, column, quads: near_source(i, -1, 1, column, quads),
    )
    total = total + upward[:COLS] + downward[:COLS]
    crossing = jnp.where(high, two + downward[COLS:], eight + upward[COLS:])
    far_sums = send(eight, lambda i, column, quads: inner_source(i, -2, column, quads))
    far_sums = far_sums + send(two, lambda i, column, quads: inner_source(i, 2, column, quads))
    total = total + send(crossing, far_source) + far_sums
    return total.T


def solution(mesh):
    return jax.shard_map(
        on_device,
        mesh=mesh,
        in_specs=(P(AXES, None), P(AXES, None)),
        out_specs=P(AXES, None),
        check_vma=False,
    )
```

```python
import functools

import jax
import jax.numpy as jnp
from jax import lax
from jax.experimental import pallas as pl
from jax.experimental.pallas import tpu as pltpu
from jax.sharding import PartitionSpec as P

WAVE = 1024
BLK = 224
COLS = 32
PACK = 16
AXES = ("gx", "gy")

spread_rate = 4.0


def split(i):
    return i >> 2, (i >> 1) & 1, i & 1


def device(quad, side, core, quads):
    return (quad % quads) * 4 + side * 2 + core


def stepped(i, j, quads):
    quad, side, core = split(i)
    return device(quad + j, side, core, quads)


def within(i, j, column, quads):
    return stepped(i, j, quads) // (4 * column) == i // (4 * column)


def near_source(i, j, steps, column, quads):
    return stepped(i, j, quads) if within(i, j * steps, column, quads) else None


def inner_source(i, j, column, quads):
    return stepped(i, j, quads) if within(i, j, column, quads) else None


def far_source(i, column, quads):
    for j in (2, -2):
        if not within(i, j, column, quads):
            return stepped(i, j, quads)
    return None


def back_level(me, column):
    level = (me >> 2) % column
    return (level == 1) | (level == column - 2)


def back_source(i, column, quads):
    for j in (1, -1):
        if not within(i, j, column, quads):
            return stepped(i, -j, quads)
    return None


def sources(source_of, n, column):
    found = [(source_of(i, column, n // 4), i) for i in range(n)]
    return [(source, i) for source, i in found if source is not None]


VMEM = pl.BlockSpec(memory_space=pltpu.VMEM)
ROW = jax.ShapeDtypeStruct((1, BLK), jnp.float32)


def packed_body(spectra_ref, scores_ref, out_ref):
    out_ref[0:BLK, :] = spectra_ref[...]
    turned = scores_ref[...].astype(jnp.float32).T.astype(jnp.bfloat16)
    out_ref[BLK:BLK + PACK, :] = jnp.zeros((PACK, WAVE), jnp.bfloat16)
    out_ref[BLK:BLK + PACK, 0:BLK] = turned[0:PACK]
    out_ref[BLK:BLK + PACK, 256:256 + BLK] = turned[PACK:COLS]


def packed(spectra, scores):
    return pl.pallas_call(
        packed_body,
        out_shape=jax.ShapeDtypeStruct((BLK + PACK, WAVE), jnp.bfloat16),
        in_specs=[VMEM] * 2,
        out_specs=VMEM,
        compiler_params=pltpu.CompilerParams(vmem_limit_bytes=12 * 1024 * 1024),
        cost_estimate=pl.CostEstimate(flops=0, bytes_accessed=4 * BLK * WAVE, transcendentals=0),
    )(spectra, scores)


def pick_body(which_ref, one_ref, other_ref, out_ref):
    @pl.when(which_ref[0] != 0)
    def _():
        out_ref[...] = one_ref[...]

    @pl.when(which_ref[0] == 0)
    def _():
        out_ref[...] = other_ref[...]


def pick(which, one, other):
    return pl.pallas_call(
        pick_body,
        out_shape=jax.ShapeDtypeStruct(one.shape, one.dtype),
        in_specs=[pl.BlockSpec(memory_space=pltpu.SMEM)] + [VMEM] * 2,
        out_specs=VMEM,
        compiler_params=pltpu.CompilerParams(vmem_limit_bytes=12 * 1024 * 1024),
        cost_estimate=pl.CostEstimate(flops=0, bytes_accessed=4 * BLK * WAVE, transcendentals=0),
    )(which.astype(jnp.int32).reshape(1), one, other)


def rows_of(ref):
    return ref[0:BLK, :]


def scores_of(ref):
    return jnp.concatenate([ref[BLK:BLK + PACK, 0:BLK], ref[BLK:BLK + PACK, 256:256 + BLK]], axis=0)


def norms_of(ref):
    x = rows_of(ref).astype(jnp.float32)
    column = jnp.sum(x * x, axis=1, keepdims=True)
    row = jnp.broadcast_to(column, (BLK, 128)).T[0:1, :]
    return column, row


def tile_of(a_ref, a_column, b_ref, b_row):
    cross = lax.dot_general(
        rows_of(a_ref), rows_of(b_ref), (((1,), (1,)), ((), ())), preferred_element_type=jnp.float32
    )
    dist = a_column + b_row - 2.0 * cross
    return jnp.exp(-spread_rate * dist / WAVE).astype(jnp.bfloat16)


def to_rows(kern, b_scores):
    return lax.dot_general(b_scores, kern, (((1,), (1,)), ((), ())), preferred_element_type=jnp.float32)


def to_columns(kern, a_scores):
    return jnp.dot(a_scores, kern, preferred_element_type=jnp.float32)


def pairs_body(tiles, outs, known, rows, *refs):
    count = len(refs) - len(outs) - len(known) - len(rows)
    blocks, before, totals = refs[:count], refs[count:count + len(known)], refs[count + len(known):]
    used = sorted({t for tile in tiles for t in tile})
    norms = {t: norms_of(blocks[t]) for t in used}
    scores = {t: scores_of(blocks[t]) for t in used}
    sums = {t: ref[...] for t, ref in zip(known, before)}

    def add(t, value):
        sums[t] = value if t not in sums else sums[t] + value

    for a, b in tiles:
        kern = tile_of(blocks[a], norms[a][0], blocks[b], norms[b][1])
        add(a, to_rows(kern, scores[b]))
        if a != b:
            add(b, to_columns(kern, scores[a]))
    for t, total in zip(outs, totals):
        total[...] = sums[t]
    for t, row in zip(rows, totals[len(outs):]):
        row[...] = norms[t][1]


def cost(tiles, blocks):
    return pl.CostEstimate(
        flops=tiles * 2 * BLK * BLK * (WAVE + 2 * COLS),
        bytes_accessed=blocks * (BLK + PACK) * WAVE * 2,
        transcendentals=tiles * BLK * BLK,
    )


def pairs(blocks, tiles, outs, known, rows, sums):
    return pl.pallas_call(
        functools.partial(pairs_body, tiles, outs, known, rows),
        out_shape=[jax.ShapeDtypeStruct((COLS, BLK), jnp.float32)] * len(outs) + [ROW] * len(rows),
        in_specs=[VMEM] * (len(blocks) + len(sums)),
        out_specs=[VMEM] * (len(outs) + len(rows)),
        compiler_params=pltpu.CompilerParams(vmem_limit_bytes=12 * 1024 * 1024),
        cost_estimate=cost(len(tiles), len(blocks)),
    )(*blocks, *sums)


def extra_body(
    low_ref, extra_ref, zero_ref, up_ref, down_ref, up2_ref, down2_ref,
    zero_norms, up_norms, down_norms, up2_norms, down2_norms,
    zero_in, up_in, down_in, up2_in, down2_in,
    zero_total, up_total, down_total, up2_total, down2_total, extra_total,
):
    column, _ = norms_of(extra_ref)
    extra_scores = scores_of(extra_ref)

    def one(ref, norms, before, after):
        kern = tile_of(extra_ref, column, ref, norms[...])
        after[...] = before[...] + to_columns(kern, extra_scores)
        return to_rows(kern, scores_of(ref))

    mine = one(zero_ref, zero_norms, zero_in, zero_total)
    mine = mine + one(up_ref, up_norms, up_in, up_total)
    extra_total[...] = mine + one(down_ref, down_norms, down_in, down_total)

    @pl.when(low_ref[0] != 0)
    def _():
        extra_total[...] += one(up2_ref, up2_norms, up2_in, up2_total)
        down2_total[...] = down2_in[...]

    @pl.when(low_ref[0] == 0)
    def _():
        extra_total[...] += one(down2_ref, down2_norms, down2_in, down2_total)
        up2_total[...] = up2_in[...]


def extra_pairs(is_low, extra, blocks, norms, sums):
    total = jax.ShapeDtypeStruct((COLS, BLK), jnp.float32)
    outs = pl.pallas_call(
        extra_body,
        out_shape=[total] * 6,
        in_specs=[pl.BlockSpec(memory_space=pltpu.SMEM)] + [VMEM] * 16,
        out_specs=[VMEM] * 6,
        compiler_params=pltpu.CompilerParams(vmem_limit_bytes=12 * 1024 * 1024),
        cost_estimate=cost(4, 6),
    )(is_low.astype(jnp.int32).reshape(1), extra, *blocks, *norms, *sums)
    return outs[:5], outs[5]


def early_body(low_ref, extra_ref, zero_ref, up2_ref, down2_ref,
               zero_total, up2_total, down2_total, extra_total, zero_norms, up2_norms, down2_norms, chosen_ref):
    low = low_ref[0] != 0

    @pl.when(low)
    def _():
        chosen_ref[...] = up2_ref[...]

    @pl.when(jnp.logical_not(low))
    def _():
        chosen_ref[...] = down2_ref[...]

    zero_column, zero_row = norms_of(zero_ref)
    zero_scores = scores_of(zero_ref)
    total = to_rows(tile_of(zero_ref, zero_column, zero_ref, zero_row), zero_scores)
    _, up2_row = norms_of(up2_ref)
    down2_column, down2_row = norms_of(down2_ref)
    zero_norms[...], up2_norms[...], down2_norms[...] = zero_row, up2_row, down2_row
    kern = tile_of(down2_ref, down2_column, up2_ref, up2_row)
    down2_sum = to_rows(kern, scores_of(up2_ref))
    up2_sum = to_columns(kern, scores_of(down2_ref))
    column, _ = norms_of(extra_ref)
    scores = scores_of(extra_ref)
    kern = tile_of(extra_ref, column, zero_ref, zero_row)
    mine = to_rows(kern, zero_scores)
    zero_total[...] = total + to_columns(kern, scores)
    kern = tile_of(extra_ref, column, chosen_ref, jnp.where(low, up2_row, down2_row))
    extra_total[...] = mine + to_rows(kern, scores_of(chosen_ref))
    theirs = to_columns(kern, scores)
    up2_total[...] = up2_sum + jnp.where(low, theirs, 0.0)
    down2_total[...] = down2_sum + jnp.where(low, 0.0, theirs)


def early_pairs(is_low, blocks):
    return pl.pallas_call(
        early_body,
        out_shape=[jax.ShapeDtypeStruct((COLS, BLK), jnp.float32)] * 4 + [ROW] * 3,
        in_specs=[pl.BlockSpec(memory_space=pltpu.SMEM)] + [VMEM] * 4,
        out_specs=[VMEM] * 7,
        scratch_shapes=[pltpu.VMEM((BLK + PACK, WAVE), jnp.bfloat16)],
        compiler_params=pltpu.CompilerParams(vmem_limit_bytes=12 * 1024 * 1024),
        cost_estimate=cost(4, 4),
    )(is_low.astype(jnp.int32).reshape(1), *blocks)


def on_device(spectra, scores):
    n = lax.axis_size(AXES)
    quads = n // 4
    me = lax.axis_index(AXES)
    column = lax.axis_size("gy") // 4
    level = (me >> 2) % column
    low, high = level < 2, level >= column - 2
    def route(block, source_of):
        return lax.ppermute(block, AXES, sources(source_of, n, column))

    def send(block, source_of):
        return lax.ppermute(block, AXES, [(i, source) for source, i in sources(source_of, n, column)])

    def swap(block, bits):
        return lax.ppermute(block, AXES, [(i, i ^ bits) for i in range(n)])

    zero = packed(spectra, scores)
    far = route(zero, far_source)
    up = route(zero, lambda i, column, quads: near_source(i, 1, 1, column, quads))
    down = route(zero, lambda i, column, quads: near_source(i, -1, 1, column, quads))
    up2 = route(up, lambda i, column, quads: near_source(i, 1, 2, column, quads))
    down2 = route(down, lambda i, column, quads: near_source(i, -1, 2, column, quads))
    back = route(jnp.where(back_level(me, column), far, up2), back_source)
    up2 = pick(high, far, up2)
    beside = swap(up2, 2)
    sibling = swap(up2, 1)
    across = swap(beside, 1)
    up2, down2 = lax.optimization_barrier((up2, down2))
    down2 = jnp.where(low, far, down2)
    back, _, _ = lax.optimization_barrier((back, up2, down2))
    up = jnp.where(level == column - 1, back, up)
    down = jnp.where(level == 0, back, down)

    total, two, eight, for_sibling, zero_norms, up2_norms, down2_norms = early_pairs(
        (me & 1) == 0, [sibling, zero, up2, down2]
    )
    total, one, nine, two, for_sibling, up_norms, down_norms = pairs(
        [zero, up, down, up2, sibling],
        ((0, 1), (2, 1), (2, 3), (4, 1), (4, 2)),
        (0, 1, 2, 3, 4),
        (0, 3, 4),
        (1, 2),
        [total, two, for_sibling],
    )
    blocks = [zero, up, down, up2, down2]
    norms = [zero_norms, up_norms, down_norms, up2_norms, down2_norms]
    sums, for_beside = extra_pairs((me & 2) == 0, beside, blocks, norms, [total, one, nine, two, eight])
    sums, for_across = extra_pairs((me & 2) == 0, across, blocks, norms, sums)
    total, one, nine, two, eight = sums
    handed = swap(jnp.concatenate([for_sibling, for_across]), 1)
    two = two + handed[:COLS] + swap(for_beside + handed[COLS:], 2)

    none = jnp.zeros_like(one)
    upward = send(
        jnp.concatenate([one, jnp.where(level == 0, nine, none)]),
        lambda i, column, quads: near_source(i, 1, 1, column, quads),
    )
    downward = send(
        jnp.concatenate([nine, jnp.where(level == column - 1, one, none)]),
        lambda i, column, quads: near_source(i, -1, 1, column, quads),
    )
    total = total + upward[:COLS] + downward[:COLS]
    crossing = jnp.where(high, two + downward[COLS:], eight + upward[COLS:])
    far_sums = send(eight, lambda i, column, quads: inner_source(i, -2, column, quads))
    far_sums = far_sums + send(two, lambda i, column, quads: inner_source(i, 2, column, quads))
    total = total + far_sums + send(crossing, far_source)
    return total.T


def solution(mesh):
    return jax.shard_map(
        on_device,
        mesh=mesh,
        in_specs=(P(AXES, None), P(AXES, None)),
        out_specs=P(AXES, None),
        check_vma=False,
    )
```

```python
import functools

import jax
import jax.numpy as jnp
from jax import lax
from jax.experimental import pallas as pl
from jax.experimental.pallas import tpu as pltpu
from jax.sharding import PartitionSpec as P

WAVE = 1024
BLK = 224
COLS = 32
PACK = 16
AXES = ("gx", "gy")

spread_rate = 4.0


def split(i):
    return i >> 2, (i >> 1) & 1, i & 1


def device(quad, side, core, quads):
    return (quad % quads) * 4 + side * 2 + core


def stepped(i, j, quads):
    quad, side, core = split(i)
    return device(quad + j, side, core, quads)


def within(i, j, column, quads):
    return stepped(i, j, quads) // (4 * column) == i // (4 * column)


def near_source(i, j, steps, column, quads):
    return stepped(i, j, quads) if within(i, j * steps, column, quads) else None


def inner_source(i, j, column, quads):
    return stepped(i, j, quads) if within(i, j, column, quads) else None


def far_source(i, column, quads):
    for j in (2, -2):
        if not within(i, j, column, quads):
            return stepped(i, j, quads)
    return None


def back_level(me, column):
    level = (me >> 2) % column
    return (level == 1) | (level == column - 2)


def back_source(i, column, quads):
    for j in (1, -1):
        if not within(i, j, column, quads):
            return stepped(i, -j, quads)
    return None


def sources(source_of, n, column):
    found = [(source_of(i, column, n // 4), i) for i in range(n)]
    return [(source, i) for source, i in found if source is not None]


VMEM = pl.BlockSpec(memory_space=pltpu.VMEM)
ROW = jax.ShapeDtypeStruct((1, BLK), jnp.float32)


def packed_body(spectra_ref, scores_ref, out_ref):
    out_ref[0:BLK, :] = spectra_ref[...]
    turned = scores_ref[...].astype(jnp.float32).T.astype(jnp.bfloat16)
    out_ref[BLK:BLK + PACK, :] = jnp.zeros((PACK, WAVE), jnp.bfloat16)
    out_ref[BLK:BLK + PACK, 0:BLK] = turned[0:PACK]
    out_ref[BLK:BLK + PACK, 256:256 + BLK] = turned[PACK:COLS]


def packed(spectra, scores):
    return pl.pallas_call(
        packed_body,
        out_shape=jax.ShapeDtypeStruct((BLK + PACK, WAVE), jnp.bfloat16),
        in_specs=[VMEM] * 2,
        out_specs=VMEM,
        compiler_params=pltpu.CompilerParams(vmem_limit_bytes=12 * 1024 * 1024),
        cost_estimate=pl.CostEstimate(flops=0, bytes_accessed=4 * BLK * WAVE, transcendentals=0),
    )(spectra, scores)


def pick_body(which_ref, one_ref, other_ref, out_ref):
    @pl.when(which_ref[0] != 0)
    def _():
        out_ref[...] = one_ref[...]

    @pl.when(which_ref[0] == 0)
    def _():
        out_ref[...] = other_ref[...]


def pick(which, one, other):
    return pl.pallas_call(
        pick_body,
        out_shape=jax.ShapeDtypeStruct(one.shape, one.dtype),
        in_specs=[pl.BlockSpec(memory_space=pltpu.SMEM)] + [VMEM] * 2,
        out_specs=VMEM,
        compiler_params=pltpu.CompilerParams(vmem_limit_bytes=12 * 1024 * 1024),
        cost_estimate=pl.CostEstimate(flops=0, bytes_accessed=4 * BLK * WAVE, transcendentals=0),
    )(which.astype(jnp.int32).reshape(1), one, other)


def rows_of(ref):
    return ref[0:BLK, :]


def scores_of(ref):
    return jnp.concatenate([ref[BLK:BLK + PACK, 0:BLK], ref[BLK:BLK + PACK, 256:256 + BLK]], axis=0)


def norms_of(ref):
    x = rows_of(ref).astype(jnp.float32)
    column = jnp.sum(x * x, axis=1, keepdims=True)
    row = jnp.broadcast_to(column, (BLK, 128)).T[0:1, :]
    return column, row


def tile_of(a_ref, a_column, b_ref, b_row):
    cross = lax.dot_general(
        rows_of(a_ref), rows_of(b_ref), (((1,), (1,)), ((), ())), preferred_element_type=jnp.float32
    )
    dist = a_column + b_row - 2.0 * cross
    return jnp.exp(-spread_rate * dist / WAVE).astype(jnp.bfloat16)


def to_rows(kern, b_scores):
    return lax.dot_general(b_scores, kern, (((1,), (1,)), ((), ())), preferred_element_type=jnp.float32)


def to_columns(kern, a_scores):
    return jnp.dot(a_scores, kern, preferred_element_type=jnp.float32)


def pairs_body(tiles, outs, known, rows, *refs):
    count = len(refs) - len(outs) - len(known) - len(rows)
    blocks, before, totals = refs[:count], refs[count:count + len(known)], refs[count + len(known):]
    used = sorted({t for tile in tiles for t in tile})
    norms = {t: norms_of(blocks[t]) for t in used}
    scores = {t: scores_of(blocks[t]) for t in used}
    sums = {t: ref[...] for t, ref in zip(known, before)}

    def add(t, value):
        sums[t] = value if t not in sums else sums[t] + value

    for a, b in tiles:
        kern = tile_of(blocks[a], norms[a][0], blocks[b], norms[b][1])
        add(a, to_rows(kern, scores[b]))
        if a != b:
            add(b, to_columns(kern, scores[a]))
    for t, total in zip(outs, totals):
        total[...] = sums[t]
    for t, row in zip(rows, totals[len(outs):]):
        row[...] = norms[t][1]


def cost(tiles, blocks):
    return pl.CostEstimate(
        flops=tiles * 2 * BLK * BLK * (WAVE + 2 * COLS),
        bytes_accessed=blocks * (BLK + PACK) * WAVE * 2,
        transcendentals=tiles * BLK * BLK,
    )


def pairs(blocks, tiles, outs, known, rows, sums):
    return pl.pallas_call(
        functools.partial(pairs_body, tiles, outs, known, rows),
        out_shape=[jax.ShapeDtypeStruct((COLS, BLK), jnp.float32)] * len(outs) + [ROW] * len(rows),
        in_specs=[VMEM] * (len(blocks) + len(sums)),
        out_specs=[VMEM] * (len(outs) + len(rows)),
        compiler_params=pltpu.CompilerParams(vmem_limit_bytes=12 * 1024 * 1024),
        cost_estimate=cost(len(tiles), len(blocks)),
    )(*blocks, *sums)


def extra_body(
    low_ref, extra_ref, zero_ref, up_ref, down_ref, up2_ref, down2_ref,
    zero_norms, up_norms, down_norms, up2_norms, down2_norms,
    zero_in, up_in, down_in, up2_in, down2_in,
    zero_total, up_total, down_total, up2_total, down2_total, extra_total,
):
    column, _ = norms_of(extra_ref)
    extra_scores = scores_of(extra_ref)

    def one(ref, norms, before, after):
        kern = tile_of(extra_ref, column, ref, norms[...])
        after[...] = before[...] + to_columns(kern, extra_scores)
        return to_rows(kern, scores_of(ref))

    mine = one(zero_ref, zero_norms, zero_in, zero_total)
    mine = mine + one(up_ref, up_norms, up_in, up_total)
    extra_total[...] = mine + one(down_ref, down_norms, down_in, down_total)

    @pl.when(low_ref[0] != 0)
    def _():
        extra_total[...] += one(up2_ref, up2_norms, up2_in, up2_total)
        down2_total[...] = down2_in[...]

    @pl.when(low_ref[0] == 0)
    def _():
        extra_total[...] += one(down2_ref, down2_norms, down2_in, down2_total)
        up2_total[...] = up2_in[...]


def extra_pairs(is_low, extra, blocks, norms, sums):
    total = jax.ShapeDtypeStruct((COLS, BLK), jnp.float32)
    outs = pl.pallas_call(
        extra_body,
        out_shape=[total] * 6,
        in_specs=[pl.BlockSpec(memory_space=pltpu.SMEM)] + [VMEM] * 16,
        out_specs=[VMEM] * 6,
        compiler_params=pltpu.CompilerParams(vmem_limit_bytes=12 * 1024 * 1024),
        cost_estimate=cost(4, 6),
    )(is_low.astype(jnp.int32).reshape(1), extra, *blocks, *norms, *sums)
    return outs[:5], outs[5]


def early_body(low_ref, extra_ref, zero_ref, up2_ref, down2_ref,
               zero_total, up2_total, down2_total, extra_total, zero_norms, up2_norms, down2_norms, chosen_ref):
    low = low_ref[0] != 0

    @pl.when(low)
    def _():
        chosen_ref[...] = up2_ref[...]

    @pl.when(jnp.logical_not(low))
    def _():
        chosen_ref[...] = down2_ref[...]

    zero_column, zero_row = norms_of(zero_ref)
    zero_scores = scores_of(zero_ref)
    total = to_rows(tile_of(zero_ref, zero_column, zero_ref, zero_row), zero_scores)
    _, up2_row = norms_of(up2_ref)
    down2_column, down2_row = norms_of(down2_ref)
    zero_norms[...], up2_norms[...], down2_norms[...] = zero_row, up2_row, down2_row
    kern = tile_of(down2_ref, down2_column, up2_ref, up2_row)
    down2_sum = to_rows(kern, scores_of(up2_ref))
    up2_sum = to_columns(kern, scores_of(down2_ref))
    column, _ = norms_of(extra_ref)
    scores = scores_of(extra_ref)
    kern = tile_of(extra_ref, column, zero_ref, zero_row)
    mine = to_rows(kern, zero_scores)
    zero_total[...] = total + to_columns(kern, scores)
    kern = tile_of(extra_ref, column, chosen_ref, jnp.where(low, up2_row, down2_row))
    extra_total[...] = mine + to_rows(kern, scores_of(chosen_ref))
    theirs = to_columns(kern, scores)
    up2_total[...] = up2_sum + jnp.where(low, theirs, 0.0)
    down2_total[...] = down2_sum + jnp.where(low, 0.0, theirs)


def early_pairs(is_low, blocks):
    return pl.pallas_call(
        early_body,
        out_shape=[jax.ShapeDtypeStruct((COLS, BLK), jnp.float32)] * 4 + [ROW] * 3,
        in_specs=[pl.BlockSpec(memory_space=pltpu.SMEM)] + [VMEM] * 4,
        out_specs=[VMEM] * 7,
        scratch_shapes=[pltpu.VMEM((BLK + PACK, WAVE), jnp.bfloat16)],
        compiler_params=pltpu.CompilerParams(vmem_limit_bytes=12 * 1024 * 1024),
        cost_estimate=cost(4, 4),
    )(is_low.astype(jnp.int32).reshape(1), *blocks)


def on_device(spectra, scores):
    n = lax.axis_size(AXES)
    quads = n // 4
    me = lax.axis_index(AXES)
    column = lax.axis_size("gy") // 4
    level = (me >> 2) % column
    low, high = level < 2, level >= column - 2
    def route(block, source_of):
        return lax.ppermute(block, AXES, sources(source_of, n, column))

    def send(block, source_of):
        return lax.ppermute(block, AXES, [(i, source) for source, i in sources(source_of, n, column)])

    def swap(block, bits):
        return lax.ppermute(block, AXES, [(i, i ^ bits) for i in range(n)])

    zero = packed(spectra, scores)
    far = route(zero, far_source)
    up = route(zero, lambda i, column, quads: near_source(i, 1, 1, column, quads))
    down = route(zero, lambda i, column, quads: near_source(i, -1, 1, column, quads))
    up2 = route(up, lambda i, column, quads: near_source(i, 1, 2, column, quads))
    down2 = route(down, lambda i, column, quads: near_source(i, -1, 2, column, quads))
    back = route(pick(back_level(me, column), far, up2), back_source)
    up2 = pick(high, far, up2)
    beside = swap(up2, 2)
    sibling = swap(up2, 1)
    across = swap(beside, 1)
    up2, down2 = lax.optimization_barrier((up2, down2))
    down2 = jnp.where(low, far, down2)
    back, _, _ = lax.optimization_barrier((back, up2, down2))
    up = jnp.where(level == column - 1, back, up)
    down = jnp.where(level == 0, back, down)

    total, two, eight, for_sibling, zero_norms, up2_norms, down2_norms = early_pairs(
        (me & 1) == 0, [sibling, zero, up2, down2]
    )
    total, one, nine, two, for_sibling, up_norms, down_norms = pairs(
        [zero, up, down, up2, sibling],
        ((0, 1), (2, 1), (2, 3), (4, 1), (4, 2)),
        (0, 1, 2, 3, 4),
        (0, 3, 4),
        (1, 2),
        [total, two, for_sibling],
    )
    blocks = [zero, up, down, up2, down2]
    norms = [zero_norms, up_norms, down_norms, up2_norms, down2_norms]
    sums, for_beside = extra_pairs((me & 2) == 0, beside, blocks, norms, [total, one, nine, two, eight])
    sums, for_across = extra_pairs((me & 2) == 0, across, blocks, norms, sums)
    total, one, nine, two, eight = sums
    handed = swap(jnp.concatenate([for_sibling, for_across]), 1)
    two = two + handed[:COLS] + swap(for_beside + handed[COLS:], 2)

    none = jnp.zeros_like(one)
    upward = send(
        jnp.concatenate([one, jnp.where(level == 0, nine, none)]),
        lambda i, column, quads: near_source(i, 1, 1, column, quads),
    )
    downward = send(
        jnp.concatenate([nine, jnp.where(level == column - 1, one, none)]),
        lambda i, column, quads: near_source(i, -1, 1, column, quads),
    )
    total = total + upward[:COLS] + downward[:COLS]
    crossing = jnp.where(high, two + downward[COLS:], eight + upward[COLS:])
    far_sums = send(eight, lambda i, column, quads: inner_source(i, -2, column, quads))
    far_sums = far_sums + send(two, lambda i, column, quads: inner_source(i, 2, column, quads))
    total = total + far_sums + send(crossing, far_source)
    return total.T


def solution(mesh):
    return jax.shard_map(
        on_device,
        mesh=mesh,
        in_specs=(P(AXES, None), P(AXES, None)),
        out_specs=P(AXES, None),
        check_vma=False,
    )
```

```python
import functools

import jax
import jax.numpy as jnp
from jax import lax
from jax.experimental import pallas as pl
from jax.experimental.pallas import tpu as pltpu
from jax.sharding import PartitionSpec as P

WAVE = 1024
BLK = 224
COLS = 32
PACK = 16
AXES = ("gx", "gy")

spread_rate = 4.0


def split(i):
    return i >> 2, (i >> 1) & 1, i & 1


def device(quad, side, core, quads):
    return (quad % quads) * 4 + side * 2 + core


def stepped(i, j, quads):
    quad, side, core = split(i)
    return device(quad + j, side, core, quads)


def within(i, j, column, quads):
    return stepped(i, j, quads) // (4 * column) == i // (4 * column)


def near_source(i, j, steps, column, quads):
    return stepped(i, j, quads) if within(i, j * steps, column, quads) else None


def inner_source(i, j, column, quads):
    return stepped(i, j, quads) if within(i, j, column, quads) else None


def far_source(i, column, quads):
    for j in (2, -2):
        if not within(i, j, column, quads):
            return stepped(i, j, quads)
    return None


def back_level(me, column):
    level = (me >> 2) % column
    return (level == 1) | (level == column - 2)


def back_source(i, column, quads):
    for j in (1, -1):
        if not within(i, j, column, quads):
            return stepped(i, -j, quads)
    return None


def sources(source_of, n, column):
    found = [(source_of(i, column, n // 4), i) for i in range(n)]
    return [(source, i) for source, i in found if source is not None]


VMEM = pl.BlockSpec(memory_space=pltpu.VMEM)
ROW = jax.ShapeDtypeStruct((1, BLK), jnp.float32)


def packed_body(spectra_ref, scores_ref, out_ref):
    out_ref[0:BLK, :] = spectra_ref[...]
    turned = scores_ref[...].astype(jnp.float32).T.astype(jnp.bfloat16)
    out_ref[BLK:BLK + PACK, :] = jnp.zeros((PACK, WAVE), jnp.bfloat16)
    out_ref[BLK:BLK + PACK, 0:BLK] = turned[0:PACK]
    out_ref[BLK:BLK + PACK, 256:256 + BLK] = turned[PACK:COLS]


def packed(spectra, scores):
    return pl.pallas_call(
        packed_body,
        out_shape=jax.ShapeDtypeStruct((BLK + PACK, WAVE), jnp.bfloat16),
        in_specs=[VMEM] * 2,
        out_specs=VMEM,
        compiler_params=pltpu.CompilerParams(vmem_limit_bytes=12 * 1024 * 1024),
        cost_estimate=pl.CostEstimate(flops=0, bytes_accessed=4 * BLK * WAVE, transcendentals=0),
    )(spectra, scores)


def pick_body(which_ref, one_ref, other_ref, out_ref):
    @pl.when(which_ref[0] != 0)
    def _():
        out_ref[...] = one_ref[...]

    @pl.when(which_ref[0] == 0)
    def _():
        out_ref[...] = other_ref[...]


def pick(which, one, other):
    return pl.pallas_call(
        pick_body,
        out_shape=jax.ShapeDtypeStruct(one.shape, one.dtype),
        in_specs=[pl.BlockSpec(memory_space=pltpu.SMEM)] + [VMEM] * 2,
        out_specs=VMEM,
        compiler_params=pltpu.CompilerParams(vmem_limit_bytes=12 * 1024 * 1024),
        cost_estimate=pl.CostEstimate(flops=0, bytes_accessed=4 * BLK * WAVE, transcendentals=0),
    )(which.astype(jnp.int32).reshape(1), one, other)


def rows_of(ref):
    return ref[0:BLK, :]


def scores_of(ref):
    return jnp.concatenate([ref[BLK:BLK + PACK, 0:BLK], ref[BLK:BLK + PACK, 256:256 + BLK]], axis=0)


def norms_of(ref):
    x = rows_of(ref).astype(jnp.float32)
    column = jnp.sum(x * x, axis=1, keepdims=True)
    row = jnp.broadcast_to(column, (BLK, 128)).T[0:1, :]
    return column, row


def tile_of(a_ref, a_column, b_ref, b_row):
    cross = lax.dot_general(
        rows_of(a_ref), rows_of(b_ref), (((1,), (1,)), ((), ())), preferred_element_type=jnp.float32
    )
    dist = a_column + b_row - 2.0 * cross
    return jnp.exp(-spread_rate * dist / WAVE).astype(jnp.bfloat16)


def to_rows(kern, b_scores):
    return lax.dot_general(b_scores, kern, (((1,), (1,)), ((), ())), preferred_element_type=jnp.float32)


def to_columns(kern, a_scores):
    return jnp.dot(a_scores, kern, preferred_element_type=jnp.float32)


def pairs_body(tiles, outs, known, rows, *refs):
    count = len(refs) - len(outs) - len(known) - len(rows)
    blocks, before, totals = refs[:count], refs[count:count + len(known)], refs[count + len(known):]
    used = sorted({t for tile in tiles for t in tile})
    norms = {t: norms_of(blocks[t]) for t in used}
    scores = {t: scores_of(blocks[t]) for t in used}
    sums = {t: ref[...] for t, ref in zip(known, before)}

    def add(t, value):
        sums[t] = value if t not in sums else sums[t] + value

    for a, b in tiles:
        kern = tile_of(blocks[a], norms[a][0], blocks[b], norms[b][1])
        add(a, to_rows(kern, scores[b]))
        if a != b:
            add(b, to_columns(kern, scores[a]))
    for t, total in zip(outs, totals):
        total[...] = sums[t]
    for t, row in zip(rows, totals[len(outs):]):
        row[...] = norms[t][1]


def cost(tiles, blocks):
    return pl.CostEstimate(
        flops=tiles * 2 * BLK * BLK * (WAVE + 2 * COLS),
        bytes_accessed=blocks * (BLK + PACK) * WAVE * 2,
        transcendentals=tiles * BLK * BLK,
    )


def pairs(blocks, tiles, outs, known, rows, sums):
    return pl.pallas_call(
        functools.partial(pairs_body, tiles, outs, known, rows),
        out_shape=[jax.ShapeDtypeStruct((COLS, BLK), jnp.float32)] * len(outs) + [ROW] * len(rows),
        in_specs=[VMEM] * (len(blocks) + len(sums)),
        out_specs=[VMEM] * (len(outs) + len(rows)),
        compiler_params=pltpu.CompilerParams(vmem_limit_bytes=12 * 1024 * 1024),
        cost_estimate=cost(len(tiles), len(blocks)),
    )(*blocks, *sums)


def extra_body(
    low_ref, extra_ref, zero_ref, up_ref, down_ref, up2_ref, down2_ref,
    zero_norms, up_norms, down_norms, up2_norms, down2_norms,
    zero_in, up_in, down_in, up2_in, down2_in,
    zero_total, up_total, down_total, up2_total, down2_total, extra_total,
):
    column, _ = norms_of(extra_ref)
    extra_scores = scores_of(extra_ref)

    def one(ref, norms, before, after):
        kern = tile_of(extra_ref, column, ref, norms[...])
        after[...] = before[...] + to_columns(kern, extra_scores)
        return to_rows(kern, scores_of(ref))

    mine = one(zero_ref, zero_norms, zero_in, zero_total)
    mine = mine + one(up_ref, up_norms, up_in, up_total)
    extra_total[...] = mine + one(down_ref, down_norms, down_in, down_total)

    @pl.when(low_ref[0] != 0)
    def _():
        extra_total[...] += one(up2_ref, up2_norms, up2_in, up2_total)
        down2_total[...] = down2_in[...]

    @pl.when(low_ref[0] == 0)
    def _():
        extra_total[...] += one(down2_ref, down2_norms, down2_in, down2_total)
        up2_total[...] = up2_in[...]


def extra_pairs(is_low, extra, blocks, norms, sums):
    total = jax.ShapeDtypeStruct((COLS, BLK), jnp.float32)
    outs = pl.pallas_call(
        extra_body,
        out_shape=[total] * 6,
        in_specs=[pl.BlockSpec(memory_space=pltpu.SMEM)] + [VMEM] * 16,
        out_specs=[VMEM] * 6,
        compiler_params=pltpu.CompilerParams(vmem_limit_bytes=12 * 1024 * 1024),
        cost_estimate=cost(4, 6),
    )(is_low.astype(jnp.int32).reshape(1), extra, *blocks, *norms, *sums)
    return outs[:5], outs[5]


def early_body(low_ref, extra_ref, zero_ref, up2_ref, down2_ref,
               zero_total, up2_total, down2_total, extra_total, zero_norms, up2_norms, down2_norms, chosen_ref):
    low = low_ref[0] != 0

    @pl.when(low)
    def _():
        chosen_ref[...] = up2_ref[...]

    @pl.when(jnp.logical_not(low))
    def _():
        chosen_ref[...] = down2_ref[...]

    zero_column, zero_row = norms_of(zero_ref)
    zero_scores = scores_of(zero_ref)
    total = to_rows(tile_of(zero_ref, zero_column, zero_ref, zero_row), zero_scores)
    _, up2_row = norms_of(up2_ref)
    down2_column, down2_row = norms_of(down2_ref)
    zero_norms[...], up2_norms[...], down2_norms[...] = zero_row, up2_row, down2_row
    kern = tile_of(down2_ref, down2_column, up2_ref, up2_row)
    down2_sum = to_rows(kern, scores_of(up2_ref))
    up2_sum = to_columns(kern, scores_of(down2_ref))
    column, _ = norms_of(extra_ref)
    scores = scores_of(extra_ref)
    kern = tile_of(extra_ref, column, zero_ref, zero_row)
    mine = to_rows(kern, zero_scores)
    zero_total[...] = total + to_columns(kern, scores)
    kern = tile_of(extra_ref, column, chosen_ref, jnp.where(low, up2_row, down2_row))
    extra_total[...] = mine + to_rows(kern, scores_of(chosen_ref))
    theirs = to_columns(kern, scores)
    up2_total[...] = up2_sum + jnp.where(low, theirs, 0.0)
    down2_total[...] = down2_sum + jnp.where(low, 0.0, theirs)


def early_pairs(is_low, blocks):
    return pl.pallas_call(
        early_body,
        out_shape=[jax.ShapeDtypeStruct((COLS, BLK), jnp.float32)] * 4 + [ROW] * 3,
        in_specs=[pl.BlockSpec(memory_space=pltpu.SMEM)] + [VMEM] * 4,
        out_specs=[VMEM] * 7,
        scratch_shapes=[pltpu.VMEM((BLK + PACK, WAVE), jnp.bfloat16)],
        compiler_params=pltpu.CompilerParams(vmem_limit_bytes=12 * 1024 * 1024),
        cost_estimate=cost(4, 4),
    )(is_low.astype(jnp.int32).reshape(1), *blocks)


def on_device(spectra, scores):
    n = lax.axis_size(AXES)
    quads = n // 4
    me = lax.axis_index(AXES)
    column = lax.axis_size("gy") // 4
    level = (me >> 2) % column
    low, high = level < 2, level >= column - 2
    def route(block, source_of):
        return lax.ppermute(block, AXES, sources(source_of, n, column))

    def send(block, source_of):
        return lax.ppermute(block, AXES, [(i, source) for source, i in sources(source_of, n, column)])

    def swap(block, bits):
        return lax.ppermute(block, AXES, [(i, i ^ bits) for i in range(n)])

    zero = packed(spectra, scores)
    far = route(zero, far_source)
    up = route(zero, lambda i, column, quads: near_source(i, 1, 1, column, quads))
    down = route(zero, lambda i, column, quads: near_source(i, -1, 1, column, quads))
    up2 = route(up, lambda i, column, quads: near_source(i, 1, 2, column, quads))
    down2 = route(down, lambda i, column, quads: near_source(i, -1, 2, column, quads))
    back = route(jnp.where(back_level(me, column), far, up2), back_source)
    up2 = pick(high, far, up2)
    beside = swap(up2, 2)
    sibling = swap(up2, 1)
    across = swap(beside, 1)
    up2, down2 = lax.optimization_barrier((up2, down2))
    down2 = pick(low, far, down2)
    back, _, _ = lax.optimization_barrier((back, up2, down2))
    up = jnp.where(level == column - 1, back, up)
    down = jnp.where(level == 0, back, down)

    total, two, eight, for_sibling, zero_norms, up2_norms, down2_norms = early_pairs(
        (me & 1) == 0, [sibling, zero, up2, down2]
    )
    total, one, nine, two, for_sibling, up_norms, down_norms = pairs(
        [zero, up, down, up2, sibling],
        ((0, 1), (2, 1), (2, 3), (4, 1), (4, 2)),
        (0, 1, 2, 3, 4),
        (0, 3, 4),
        (1, 2),
        [total, two, for_sibling],
    )
    blocks = [zero, up, down, up2, down2]
    norms = [zero_norms, up_norms, down_norms, up2_norms, down2_norms]
    sums, for_beside = extra_pairs((me & 2) == 0, beside, blocks, norms, [total, one, nine, two, eight])
    sums, for_across = extra_pairs((me & 2) == 0, across, blocks, norms, sums)
    total, one, nine, two, eight = sums
    handed = swap(jnp.concatenate([for_sibling, for_across]), 1)
    two = two + handed[:COLS] + swap(for_beside + handed[COLS:], 2)

    none = jnp.zeros_like(one)
    upward = send(
        jnp.concatenate([one, jnp.where(level == 0, nine, none)]),
        lambda i, column, quads: near_source(i, 1, 1, column, quads),
    )
    downward = send(
        jnp.concatenate([nine, jnp.where(level == column - 1, one, none)]),
        lambda i, column, quads: near_source(i, -1, 1, column, quads),
    )
    total = total + upward[:COLS] + downward[:COLS]
    crossing = jnp.where(high, two + downward[COLS:], eight + upward[COLS:])
    far_sums = send(eight, lambda i, column, quads: inner_source(i, -2, column, quads))
    far_sums = far_sums + send(two, lambda i, column, quads: inner_source(i, 2, column, quads))
    total = total + far_sums + send(crossing, far_source)
    return total.T


def solution(mesh):
    return jax.shard_map(
        on_device,
        mesh=mesh,
        in_specs=(P(AXES, None), P(AXES, None)),
        out_specs=P(AXES, None),
        check_vma=False,
    )
```
